128 devices in a mesh: tile: 32 (over y, z, core), net: 4 (over x).
Axes of the slice: x: 4, y: 4, z: 4, core: 2. Of those that a mesh axis runs over, the one named last changes fastest.
Arguments:
- seg_start: float32 [16384, 128], P(('tile', 'net')), may hold values from 0 to 8
- seg_len: float32 [16384, 128], P(('tile', 'net')), may hold values from 0.25 to 2
- seg_track: float32 [16384, 128], P(('tile', 'net')), may hold values from -1 to 1
- seg_nbr: int32 [16384, 4], P(('tile', 'net')), may hold values from 0 to 16383, as said below
- seg_owner: int32 [16384, 128, 1], P(('tile', 'net')), may hold values from 0 to 127; in each aligned block of 16384 rows (0 to 16383, 16384 to 32767, ..., all dimensions but the last counted through in order) at most 256 rows name the same one
- seg_local: int32 [16384, 128], P(('tile', 'net')), may hold values from 0 to 511
- seg_node: int32 [16384, 128], P(('tile', 'net')), may hold values from 0 to 31
- pin_res: float32 [32, 65536], P(None, ('tile', 'net')), may hold values from 0.02 to 0.2
- load_cap: float32 [32, 65536], P(None, ('tile', 'net')), may hold values from 0.1 to 1
- crit_weight: float32 [32, 65536], P(None, ('tile', 'net')), may hold values from 0.1 to 1
- net_parent: int32 [32, 65536], P(None, ('tile', 'net')), may hold values from -1 to 30, as said below
Outputs:
- seg_cap: float32 [16384, 128], P(('tile', 'net'))
- delay: float32 [32, 65536], P(None, ('tile', 'net'))
- seg_sens: float32 [16384, 128], P(('tile', 'net'))
The draws below stay inside these ranges and needn't reach their ends.
Inputs may be any that keep to these rules, and one draw needn't show every extreme that they name: `seg_nbr`: each listed block is another block within 4 blocks of the listing block; the first listed block of every block lies exactly 4 blocks away. `seg_owner`: among the segments of one device at most 256 name any one owner, and in some device one owner is named exactly 256 times. `net_parent`: node 0 of each net has parent -1; every other node's parent has a smaller index.
All inputs are finite; a program needn't handle non-finite values.
Results may differ from the reference program's by a relative error of at most 0.0003.
Values sent between devices are 32-bit elements; how exact they have to be, the bound alone decides.
No kernel may reach another device: no remote copies, remote signals or barrier semaphores. Data moves between devices by JAX's collectives and lax.ppermute only.
A program may use at most 128 MiB of HBM per device.

```python
import math
import jax
import jax.numpy as jnp
import numpy as np
from jax import lax

SBLK = 128
NBR = 4
RIM = 4
NODES = 32
NET_DEV = 512
NBLK = 16384
NETS = 65536
CAPS = 256
DEVICES = 128


def draw_seg_nbr(key, part):
    block_index = jnp.arange(NBLK, dtype=jnp.int32)[:, None]
    key_size, key_side = jax.random.split(key)
    magnitude = jax.random.randint(key_size, (NBLK, NBR), 1, RIM + 1, dtype=jnp.int32)
    magnitude = magnitude.at[:, 0].set(RIM)
    side_sign = jax.random.randint(key_side, (NBLK, NBR), 0, 2, dtype=jnp.int32) * 2 - 1
    offset = side_sign * magnitude
    target = block_index + offset
    return jnp.where((target < 0) | (target >= NBLK), block_index - offset, target).astype(jnp.int32)


def draw_net_parent(key, part):
    node_index = jnp.arange(NODES, dtype=jnp.int32)[:, None]
    step_back = jax.random.randint(key, (NODES, NETS), 1, 5, dtype=jnp.int32)
    parent_of = jnp.maximum(node_index - step_back, 0)
    return jnp.where(node_index == 0, -1, parent_of).astype(jnp.int32)


def touch_ends(drawn, rng, least, top_value):
    longest = drawn.shape.index(max(drawn.shape))
    spots = []
    for shift in (0, 1):
        where = [jax.random.randint(jax.random.fold_in(rng, axis), (), 0, length) for axis, length in enumerate(drawn.shape)]
        where[longest] = (where[longest] + shift) % drawn.shape[longest]
        spots.append(tuple(where))
    return drawn.at[spots[0]].set(least).at[spots[1]].set(top_value)


def block_levels(rng, dims, cuts, smallest, high):
    def one(dim, shards_of):
        heights = jax.random.uniform(jax.random.fold_in(jax.random.fold_in(rng, 6), dim), (shards_of,), jnp.float32, smallest / len(cuts), high / len(cuts))
        return jnp.repeat(jnp.exp(heights), dims[dim] // shards_of).reshape((-1,) + (1,) * (len(dims) - dim - 1))

    loudness = one(*cuts[0])
    for cut in cuts[1:]:
        loudness = loudness * one(*cut)
    return loudness


def routed_block(stream_key, own, number, rows, amount, top, limit, skew):
    order = jax.random.permutation(stream_key, amount)
    crowded, usual = shares(amount, rows * top, limit, skew, True), shares(amount, rows * top, limit, skew, False)
    places = jnp.arange(amount)

    def named(sizes, turn):
        used = int((sizes > 0).sum())
        fixed = max(1, used // 4)
        shifted = fixed + (places - fixed + turn * (used - fixed)) % max(1, amount - fixed)
        return jnp.zeros((amount,), jnp.int32).at[order[jnp.where(places < fixed, places, shifted)]].set(jnp.asarray(sizes, jnp.int32))

    sizes = jnp.where(number % 4 == 0, named(crowded, number // 4), named(usual, number - number // 4 - 1))
    mixed = jax.random.permutation(jax.random.fold_in(own, 3), amount)
    donor, receiver = mixed[0:amount // 2 * 2:2], mixed[1:amount // 2 * 2:2]
    slack = jnp.minimum(sizes[donor] - 1, limit - sizes[receiver]) // 2
    slack = jnp.where((donor == order[0]) | (receiver == order[0]) | (sizes[receiver] == 0), 0, jnp.maximum(slack, 0))
    shifted = jax.random.randint(jax.random.fold_in(own, 4), (amount // 2,), 0, 1 << 20) % (slack + 1)
    sizes = sizes.at[donor].add(-shifted).at[receiver].add(shifted)
    items = jnp.searchsorted(jnp.cumsum(sizes), jnp.arange(rows * top), side="right").astype(jnp.int32)
    listing = items.reshape(top, rows).T
    listing = listing[jax.random.permutation(jax.random.fold_in(own, 1), rows)]
    turn = jax.random.randint(jax.random.fold_in(own, 2), (rows, 1), 0, top)
    return jnp.take_along_axis(listing, (jnp.arange(top)[None, :] + turn) % top, axis=1)


def shares(amount, total, reach, skew, full):
    portions = [(1 << 20) // math.isqrt(standing ** skew) + 1 for standing in range(1, amount + 1)]
    largest = reach if full else min(reach, max(-(-total // amount), total * portions[0] // sum(portions)))
    least = 1 if total - largest >= amount - 1 else 0
    counts, surplus = [largest] + [least] * (amount - 1), total - largest - least * (amount - 1)
    while surplus > 0:
        free = [i for i in range(1, amount) if counts[i] < largest] or [i for i in range(1, amount) if counts[i] < reach]
        pool, remaining = sum([portions[i] for i in free]), surplus
        for i in free:
            extra = min(reach - counts[i], max(1, remaining * portions[i] // pool), surplus)
            counts[i] = counts[i] + extra
            surplus = surplus - extra
    return np.array(counts)


def setup_inputs(seed: int = 0) -> dict:
    arg_keys = jax.random.split(jax.random.key(seed), 12)
    seg_start = jnp.clip(8.0 * jax.random.uniform(arg_keys[0], (NBLK, 128), jnp.float32) ** block_levels(arg_keys[0], (NBLK, 128), ((0, 128),), -0.2, 0.2), 0.0, 8.0)
    seg_len = jnp.clip(jnp.exp(math.log(2.0) - 2.0794415 * jax.random.uniform(arg_keys[1], (NBLK, 128), jnp.float32) ** block_levels(arg_keys[1], (NBLK, 128), ((0, 128),), -0.2, 0.2)), 0.25, 2.0)
    seg_track = jnp.clip(jax.random.uniform(arg_keys[2], (NBLK, 128), jnp.float32, -1.0, 1.0) * block_levels(arg_keys[2], (NBLK, 128), ((0, 128),), -0.4, 0.0), -1.0, 1.0)
    seg_nbr = draw_seg_nbr(jax.random.fold_in(arg_keys[11], 71), 0)
    seg_owner_keys = jax.random.split(jax.random.fold_in(arg_keys[4], 1), NBLK * 128 // (SBLK * 128))
    seg_owner_turns = jax.random.permutation(jax.random.fold_in(arg_keys[4], 3), NBLK * 128 // (SBLK * 128))
    seg_owner = jax.vmap(lambda own, number: routed_block(jax.random.fold_in(arg_keys[4], 2), own, number, SBLK * 128, DEVICES, 1, CAPS, 2))(seg_owner_keys, seg_owner_turns).reshape((NBLK, 128, 1))
    seg_local = touch_ends(jax.random.randint(arg_keys[5], (NBLK, 128), 0, NET_DEV), jax.random.fold_in(arg_keys[5], 1), 0, NET_DEV - 1).astype(jnp.int32)
    seg_node = touch_ends(jax.random.randint(arg_keys[6], (NBLK, 128), 0, NODES), jax.random.fold_in(arg_keys[6], 1), 0, NODES - 1).astype(jnp.int32)
    pin_res = jnp.clip(jnp.exp(math.log(0.2) - 2.3025851 * jax.random.uniform(arg_keys[7], (NODES, NETS), jnp.float32) ** block_levels(arg_keys[7], (NODES, NETS), ((1, 128),), -0.2, 0.2)), 0.02, 0.2)
    load_cap = jnp.clip(jnp.exp(math.log(1.0) - 2.3025851 * jax.random.uniform(arg_keys[8], (NODES, NETS), jnp.float32) ** block_levels(arg_keys[8], (NODES, NETS), ((1, 128),), -0.2, 0.2)), 0.1, 1.0)
    crit_weight = jnp.clip(jnp.exp(math.log(1.0) - 2.3025851 * jax.random.uniform(arg_keys[9], (NODES, NETS), jnp.float32) ** block_levels(arg_keys[9], (NODES, NETS), ((1, 128),), -0.2, 0.2)), 0.1, 1.0)
    net_parent = draw_net_parent(jax.random.fold_in(arg_keys[11], 71), 0)
    return {"seg_start": seg_start, "seg_len": seg_len, "seg_track": seg_track, "seg_nbr": seg_nbr, "seg_owner": seg_owner, "seg_local": seg_local, "seg_node": seg_node, "pin_res": pin_res, "load_cap": load_cap, "crit_weight": crit_weight, "net_parent": net_parent}


GROUND = 0.2
COUPLE = 0.005
SHEET = 0.02


def couple(own_feats, near_feats):
    start_i = own_feats[:, 0, :, None]
    end_i = start_i + own_feats[:, 1, :, None]
    track_i = own_feats[:, 2, :, None]
    start_j = near_feats[:, 0, None, :]
    end_j = start_j + near_feats[:, 1, None, :]
    track_j = near_feats[:, 2, None, :]
    common_len = jnp.maximum(jnp.minimum(end_i, end_j) - jnp.maximum(start_i, start_j), 0.0)
    return COUPLE * jnp.sum(common_len * jnp.exp(-jnp.abs(track_i - track_j)), axis=2)


def matmul_batch(left, right):
    return jnp.einsum("ijn,jkn->ikn", left, right, precision=lax.Precision.HIGHEST)


def elmore(parent_of, node_cap, node_res, weight):
    node_count = parent_of.shape[0]
    node_index = jnp.arange(node_count, dtype=jnp.int32)
    step_mat = (parent_of[None, :, :] == node_index[:, None, None]).astype(node_cap.dtype)
    identity = (node_index[:, None] == node_index[None, :]).astype(node_cap.dtype)[:, :, None]
    path_mat = identity + step_mat
    power_mat = step_mat
    for level in range(node_count.bit_length() - 2):
        power_mat = matmul_batch(power_mat, power_mat)
        path_mat = path_mat + matmul_batch(path_mat, power_mat)
    highest = lax.Precision.HIGHEST
    subtree = jnp.einsum("akn,kn->an", path_mat, node_cap, precision=highest)
    delay = jnp.einsum("akn,an->kn", path_mat, node_res * subtree, precision=highest)
    below = jnp.einsum("akn,kn->an", path_mat, weight, precision=highest)
    grad_cap = jnp.einsum("akn,an->kn", path_mat, node_res * below, precision=highest)
    grad_res = below * subtree
    return delay, grad_cap, grad_res


def reference(seg_start, seg_len, seg_track, seg_nbr, seg_owner, seg_local, seg_node, pin_res, load_cap, crit_weight, net_parent):
    feats = jnp.stack([seg_start, seg_len, seg_track], axis=1)
    block_count = feats.shape[0]
    group_size = math.gcd(block_count, 64)

    def one_group(index):
        first_row = index * group_size
        own_feats = lax.dynamic_slice_in_dim(feats, first_row, group_size, 0)
        own_nbr = lax.dynamic_slice_in_dim(seg_nbr, first_row, group_size, 0)
        running = jnp.zeros((group_size, 128), feats.dtype)
        for neighbour in range(NBR):
            running = running + couple(own_feats, feats[own_nbr[:, neighbour]])
        return running

    coupling = lax.map(one_group, jnp.arange(block_count // group_size, dtype=jnp.int32)).reshape(block_count, 128)
    seg_cap = GROUND * seg_len + coupling

    owner_of = seg_owner[:, :, 0]
    flat_slot = (seg_node * NETS + owner_of * NET_DEV + seg_local).reshape(-1).astype(jnp.int32)
    slot_count = NODES * NETS
    node_cap = load_cap + jax.ops.segment_sum(seg_cap.reshape(-1), flat_slot, slot_count).reshape(NODES, NETS)
    node_res = pin_res + jax.ops.segment_sum((SHEET * seg_len).reshape(-1), flat_slot, slot_count).reshape(NODES, NETS)

    def one_shard(index):
        first_net = index * NET_DEV
        pieces = [lax.dynamic_slice_in_dim(array, first_net, NET_DEV, 1) for array in (net_parent, node_cap, node_res, crit_weight)]
        return elmore(pieces[0], pieces[1], pieces[2], pieces[3])

    delay_g, grad_cap_g, grad_res_g = lax.map(one_shard, jnp.arange(DEVICES, dtype=jnp.int32))

    def unshard(array):
        return jnp.transpose(array, (1, 0, 2)).reshape(NODES, NETS)

    delay = unshard(delay_g)
    grad_cap = unshard(grad_cap_g).reshape(-1)
    grad_res = unshard(grad_res_g).reshape(-1)
    seg_sens = (SHEET * grad_res[flat_slot] + GROUND * grad_cap[flat_slot]).reshape(block_count, 128)
    return seg_cap, delay, seg_sens
```

```python
import jax
import jax.numpy as jnp
from jax import lax
from jax.experimental import pallas as pl
from jax.experimental.pallas import tpu as pltpu
from jax.sharding import PartitionSpec as P

RIM = 4
GROUND = 0.2
COUPLE = 0.005
SHEET = 0.02
AXES = ("tile", "net")
BF = jnp.bfloat16
F32 = jnp.float32

ROWS = 128
SEG = 128
CAPS = 256
NODES = 32
HALF = 256
VMEM_LIMIT = 48 * 1024 * 1024

NT = (((1,), (1,)), ((), ()))
NN = (((1,), (0,)), ((), ()))


def mm(left, right, dims):
    return lax.dot_general(left, right, dims, preferred_element_type=F32)


def iota_bf(rows, cols):
    return lax.broadcasted_iota(jnp.int32, (rows, cols), 0).astype(F32).astype(BF)


def spread(row, rows):
    sixteen = jnp.broadcast_to(row, (16, row.shape[1])).astype(BF)
    return jnp.concatenate([sixteen] * (rows // 16), axis=0)


def split(value):
    high = value.astype(BF).astype(F32)
    return high, (value - high).astype(BF).astype(F32)


def rank_kernel(owner_ref, rank_ref):
    iota = lax.broadcasted_iota(jnp.int32, (ROWS, SEG), 0)
    r0 = lax.broadcasted_iota(jnp.int32, (SEG, 2 * SEG), 0)
    c0 = lax.broadcasted_iota(jnp.int32, (SEG, 2 * SEG), 1)
    upper = jnp.where((r0 <= c0), 1.0, 0.0).astype(BF)

    def step(g, before):
        for j in range(8):
            b = g * 8 + j
            hit = iota == owner_ref[pl.ds(b, 1), :]
            ones = jnp.where(hit, 1.0, 0.0).astype(BF)
            sums = mm(ones, upper, NN)
            placed = jnp.where(hit, sums[:, :SEG] + before, 0.0)
            rank_ref[pl.ds(b, 1), :] = jnp.sum(placed, axis=0, keepdims=True) - 1.0
            before = before + sums[:, SEG:]
        return before

    lax.fori_loop(0, ROWS // 8, step, jnp.zeros((ROWS, SEG), F32))


def couple_kernel(first_ref, nbr_ref, start_ref, len_ref, track_ref, low_ref, high_ref, out_ref,
                  s_j, e_j, g_j, f_j, s_t, e_t, g_t, res_t):
    def fill(at, count, start, length, track):
        s_j[pl.ds(at, count), :] = start
        e_j[pl.ds(at, count), :] = start + length
        g_j[pl.ds(at, count), :] = jnp.exp(2.0 * track)
        f_j[pl.ds(at, count), :] = jnp.exp(-track)

    start, length, track = start_ref[...], len_ref[...], track_ref[...]
    fill(8, ROWS, start, length, track)
    fill(0, 8, low_ref[0:8, :], low_ref[8:16, :], low_ref[16:24, :])
    fill(8 + ROWS, 8, high_ref[0:8, :], high_ref[8:16, :], high_ref[16:24, :])
    s_t[...] = start.T
    e_t[...] = (start + length).T
    g_t[...] = jnp.exp(2.0 * track).T
    lane = lax.broadcasted_iota(jnp.int32, (8, SEG), 1)
    first = first_ref[0]

    def step(b, carry):
        column = jnp.full((8, SEG), b, jnp.int32)
        rows = []
        for k in range(4):
            near = jnp.clip(nbr_ref[b, k] - first + 8, 0, ROWS + 15)
            rows.append([
                jnp.broadcast_to(ref[pl.ds(near, 1), :], (8, SEG)) for ref in (s_j, e_j, g_j, f_j)
            ])
        for t in range(SEG // 8):
            part = slice(8 * t, 8 * t + 8)
            si = jnp.take_along_axis(s_t[part, :], column, axis=1)
            ei = jnp.take_along_axis(e_t[part, :], column, axis=1)
            gi = jnp.take_along_axis(g_t[part, :], column, axis=1)
            total = None
            for sj, ej, gj, fj in rows:
                common = jnp.maximum(jnp.minimum(ei, ej) - jnp.maximum(si, sj), 0.0)
                term = common * (jnp.minimum(gi, gj) * fj)
                total = term if total is None else total + term
            summed = jnp.sum(total, axis=1, keepdims=True)
            res_t[part, :] = jnp.where(lane == b, summed, res_t[part, :])
        return carry

    lax.fori_loop(0, ROWS, step, 0)
    out_ref[...] = GROUND * length + COUPLE * f_j[8:8 + ROWS, :] * res_t[...].T


def outbox_kernel(owner_ref, rank_ref, cap_ref, len_ref, local_ref, node_ref, out_ref,
                  own, pieces, left, right, acc):
    own[...] = owner_ref[...].astype(F32)
    local, node = local_ref[...], node_ref[...]
    cap_hi, cap_lo = split(cap_ref[...])
    res_hi, res_lo = split(SHEET * len_ref[...])
    upper = (local >> 8) * NODES + node
    values = [cap_hi, cap_lo, res_hi, res_lo,
              (upper * HALF).astype(F32), (local & (HALF - 1)).astype(F32)]
    for p, value in enumerate(values):
        pieces[p * ROWS:(p + 1) * ROWS, :] = value
    acc[...] = jnp.zeros_like(acc)
    iota_o = iota_bf(ROWS, SEG)
    iota_r = iota_bf(CAPS, SEG)
    zero, one = jnp.zeros((), BF), jnp.ones((), BF)

    def step(g, carry):
        for j in range(8):
            b = g * 8 + j
            lanes = slice(j * SEG, (j + 1) * SEG)
            hit = iota_o == spread(own[pl.ds(b, 1), :], ROWS)
            for p in range(6):
                value = spread(pieces[pl.ds(p * ROWS + b, 1), :], ROWS)
                left[p * ROWS:(p + 1) * ROWS, lanes] = jnp.where(hit, value, zero)
            right[:, lanes] = jnp.where(iota_r == spread(rank_ref[pl.ds(b, 1), :], CAPS), one, zero)
        acc[...] += mm(left[...], right[...], NT)
        return carry

    lax.fori_loop(0, ROWS // 8, step, 0)
    for v in range(3):
        high = acc[2 * v * ROWS:(2 * v + 1) * ROWS, :]
        low = acc[(2 * v + 1) * ROWS:(2 * v + 2) * ROWS, :]
        out_ref[:, v * CAPS:(v + 1) * CAPS] = high + low


def owner_kernel(inbox_ref, pin_ref, load_ref, weight_ref, parent_ref, delay_ref, reply_ref,
                 upper_s, lower_s, pieces, left, right, acc):
    slot = inbox_ref[:, 2 * CAPS:].astype(jnp.int32)
    upper_s[...] = (slot >> 8).astype(F32)
    lower_s[...] = (slot & (HALF - 1)).astype(F32)
    for v in range(2):
        high, low = split(inbox_ref[:, v * CAPS:(v + 1) * CAPS])
        pieces[2 * v * ROWS:(2 * v + 1) * ROWS, :] = high
        pieces[(2 * v + 1) * ROWS:(2 * v + 2) * ROWS, :] = low
    acc[...] = jnp.zeros_like(acc)
    iota_u = iota_bf(64, CAPS)
    iota_l = iota_bf(HALF, CAPS)
    zero, one = jnp.zeros((), BF), jnp.ones((), BF)

    def collect(g, carry):
        for j in range(4):
            s = g * 4 + j
            lanes = slice(j * CAPS, (j + 1) * CAPS)
            hit = iota_u == spread(upper_s[pl.ds(s, 1), :], 64)
            for p in range(4):
                value = spread(pieces[pl.ds(p * ROWS + s, 1), :], 64)
                left[p * 64:(p + 1) * 64, lanes] = jnp.where(hit, value, zero)
            right[:, lanes] = jnp.where(iota_l == spread(lower_s[pl.ds(s, 1), :], HALF), one, zero)
        acc[...] += mm(left[...], right[...], NT)
        return carry

    lax.fori_loop(0, ROWS // 4, collect, 0)

    def table(at):
        both = acc[at:at + 64, :] + acc[at + 64:at + 128, :]
        return jnp.concatenate([both[:NODES], both[NODES:]], axis=1)

    cap = load_ref[...] + table(0)
    res = pin_ref[...] + table(128)
    weight = weight_ref[...]
    iota8 = lax.broadcasted_iota(jnp.int32, (8, 2 * HALF), 0)
    tiles = NODES // 8
    cut = lambda a: [a[8 * t:8 * t + 8, :] for t in range(tiles)]
    sub, below, res = cut(cap), cut(weight), cut(res)
    for k in range(NODES - 1, 0, -1):
        t, r = divmod(k, 8)
        parent = jnp.broadcast_to(parent_ref[k:k + 1, :], iota8.shape)
        sub_k = jnp.broadcast_to(sub[t][r:r + 1, :], iota8.shape)
        below_k = jnp.broadcast_to(below[t][r:r + 1, :], iota8.shape)
        for a in range((k - 1) // 8 + 1):
            hit = parent == iota8 + 8 * a
            sub[a] = sub[a] + jnp.where(hit, sub_k, 0.0)
            below[a] = below[a] + jnp.where(hit, below_k, 0.0)
    step_d = [res[t] * sub[t] for t in range(tiles)]
    step_g = [res[t] * below[t] for t in range(tiles)]
    down_d, down_g = list(step_d), list(step_g)
    for k in range(1, NODES):
        t, r = divmod(k, 8)
        parent = jnp.broadcast_to(parent_ref[k:k + 1, :], iota8.shape)
        from_d = from_g = None
        for a in range((k - 1) // 8 + 1):
            hit = parent == iota8 + 8 * a
            d, g = jnp.where(hit, down_d[a], 0.0), jnp.where(hit, down_g[a], 0.0)
            from_d = d if from_d is None else from_d + d
            from_g = g if from_g is None else from_g + g
        here = iota8 == r
        down_d[t] = jnp.where(here, step_d[t] + jnp.sum(from_d, axis=0, keepdims=True), down_d[t])
        down_g[t] = jnp.where(here, step_g[t] + jnp.sum(from_g, axis=0, keepdims=True), down_g[t])
    delay_ref[...] = jnp.concatenate(down_d, axis=0)
    sens = jnp.concatenate(
        [SHEET * (below[t] * sub[t]) + GROUND * down_g[t] for t in range(tiles)], axis=0)
    high, low = split(sens)
    picks = jnp.concatenate(
        [high[:, :HALF], high[:, HALF:], low[:, :HALF], low[:, HALF:]], axis=0).astype(BF)
    iota_uf = lax.broadcasted_iota(jnp.int32, (64, CAPS), 0).astype(F32)

    def answer(g, carry):
        for j in range(4):
            s = g * 4 + j
            ones = jnp.where(iota_l == spread(lower_s[pl.ds(s, 1), :], HALF), one, zero)
            found = mm(picks, ones, NN)
            kept = jnp.where(iota_uf == upper_s[pl.ds(s, 1), :], found[:64] + found[64:], 0.0)
            reply_ref[pl.ds(s, 1), :] = jnp.sum(kept, axis=0, keepdims=True)
        return carry

    lax.fori_loop(0, ROWS // 4, answer, 0)


def final_kernel(returned_ref, owner_ref, rank_ref, out_ref):
    high, low = split(returned_ref[...])
    picks = jnp.concatenate([high, low], axis=0).astype(BF)
    iota_r = iota_bf(CAPS, 2 * SEG)
    iota_o = lax.broadcasted_iota(jnp.int32, (ROWS, 2 * SEG), 0)
    zero, one = jnp.zeros((), BF), jnp.ones((), BF)

    def pair(ref, b):
        return jnp.concatenate([ref[pl.ds(b, 1), :], ref[pl.ds(b + 1, 1), :]], axis=1)

    def step(g, carry):
        for j in range(0, 8, 2):
            b = g * 8 + j
            ones = jnp.where(iota_r == spread(pair(rank_ref, b), CAPS), one, zero)
            found = mm(picks, ones, NN)
            kept = jnp.where(iota_o == pair(owner_ref, b), found[:ROWS] + found[ROWS:], 0.0)
            row = jnp.sum(kept, axis=0, keepdims=True)
            out_ref[pl.ds(b, 1), :] = row[:, :SEG]
            out_ref[pl.ds(b + 1, 1), :] = row[:, SEG:]
        return carry

    lax.fori_loop(0, ROWS // 8, step, 0)


def call(kernel, name, shapes, in_specs, scratch=()):
    vmem = pl.BlockSpec(memory_space=pltpu.VMEM)
    smem = pl.BlockSpec(memory_space=pltpu.SMEM)
    specs = [smem if c == "s" else vmem for c in in_specs]
    outs = [jax.ShapeDtypeStruct(shape, F32) for shape in shapes]
    single = len(outs) == 1
    return pl.pallas_call(
        kernel,
        out_shape=outs[0] if single else outs,
        in_specs=specs,
        out_specs=vmem if single else [vmem] * len(outs),
        scratch_shapes=[pltpu.VMEM(shape, dtype) for shape, dtype in scratch],
        compiler_params=pltpu.CompilerParams(vmem_limit_bytes=VMEM_LIMIT),
        name=name,
    )


def exchange(box):
    return lax.all_to_all(box, AXES, split_axis=0, concat_axis=0, tiled=True)


def body(seg_start, seg_len, seg_track, seg_nbr, seg_owner, seg_local, seg_node,
         pin_res, load_cap, crit_weight, net_parent):
    devices = lax.axis_size(AXES)
    forward = [(i, i + 1) for i in range(devices - 1)]
    backward = [(i + 1, i) for i in range(devices - 1)]
    feats = (seg_start, seg_len, seg_track)
    low = lax.ppermute(jnp.concatenate([f[-8:] for f in feats], axis=0), AXES, forward)
    high = lax.ppermute(jnp.concatenate([f[:8] for f in feats], axis=0), AXES, backward)
    owner = seg_owner.reshape(ROWS, SEG)
    square, flat = (ROWS, SEG), (ROWS, CAPS)
    rank = call(rank_kernel, "rank", [square], "v")(owner)
    first = (lax.axis_index(AXES) * ROWS).astype(jnp.int32).reshape(1)
    wide = (ROWS + 16, SEG)
    seg_cap = call(
        couple_kernel, "couple", [square], "ssvvvvv",
        [(wide, F32)] * 4 + [(square, F32)] * 4,
    )(first, seg_nbr, seg_start, seg_len, seg_track, low, high)
    outbox = call(
        outbox_kernel, "outbox", [(ROWS, 3 * CAPS)], "vvvvvv",
        [(square, F32), ((6 * ROWS, SEG), F32), ((6 * ROWS, 8 * SEG), BF), ((CAPS, 8 * SEG), BF),
         ((6 * ROWS, CAPS), F32)],
    )(owner, rank, seg_cap, seg_len, seg_local, seg_node)
    inbox = exchange(outbox)
    delay, reply = call(
        owner_kernel, "owner", [(NODES, 2 * HALF), flat], "vvvvv",
        [(flat, F32), (flat, F32), ((4 * ROWS, CAPS), F32), ((CAPS, 4 * CAPS), BF),
         ((HALF, 4 * CAPS), BF), ((CAPS, HALF), F32)],
    )(inbox, pin_res, load_cap, crit_weight, net_parent)
    returned = exchange(reply)
    seg_sens = call(final_kernel, "final", [square], "vvv")(returned, owner, rank)
    return seg_cap, delay, seg_sens


def solution(mesh):
    rows, nets = P(AXES, None), P(None, AXES)
    placed = (rows, rows, rows, rows, P(AXES, None, None), rows, rows, nets, nets, nets, nets)
    return jax.shard_map(body, mesh=mesh, in_specs=placed, out_specs=(rows, nets, rows), check_vma=False)
```

```python
import jax
import jax.numpy as jnp
from jax import lax
from jax.experimental import pallas as pl
from jax.experimental.pallas import tpu as pltpu
from jax.sharding import PartitionSpec as P

RIM = 4
GROUND = 0.2
COUPLE = 0.005
SHEET = 0.02
AXES = ("tile", "net")
BF = jnp.bfloat16
F32 = jnp.float32

ROWS = 128
SEG = 128
CAPS = 256
NODES = 32
HALF = 256
VMEM_LIMIT = 48 * 1024 * 1024

NT = (((1,), (1,)), ((), ()))
NN = (((1,), (0,)), ((), ()))


def mm(left, right, dims):
    return lax.dot_general(left, right, dims, preferred_element_type=F32)


def iota_bf(rows, cols):
    return lax.broadcasted_iota(jnp.int32, (rows, cols), 0).astype(F32).astype(BF)


def spread(row, rows):
    sixteen = jnp.broadcast_to(row, (16, row.shape[1])).astype(BF)
    return jnp.concatenate([sixteen] * (rows // 16), axis=0)


def split(value):
    high = value.astype(BF).astype(F32)
    return high, (value - high).astype(BF).astype(F32)


def rank_kernel(owner_ref, rank_ref):
    iota = lax.broadcasted_iota(jnp.int32, (ROWS, SEG), 0)
    r0 = lax.broadcasted_iota(jnp.int32, (SEG, 2 * SEG), 0)
    c0 = lax.broadcasted_iota(jnp.int32, (SEG, 2 * SEG), 1)
    upper = jnp.where((r0 <= c0), 1.0, 0.0).astype(BF)

    def step(g, before):
        for j in range(8):
            b = g * 8 + j
            hit = iota == owner_ref[pl.ds(b, 1), :]
            ones = jnp.where(hit, 1.0, 0.0).astype(BF)
            sums = mm(ones, upper, NN)
            placed = jnp.where(hit, sums[:, :SEG] + before, 0.0)
            rank_ref[pl.ds(b, 1), :] = jnp.sum(placed, axis=0, keepdims=True) - 1.0
            before = before + sums[:, SEG:]
        return before

    lax.fori_loop(0, ROWS // 8, step, jnp.zeros((ROWS, SEG), F32))


def split3(value):
    high = value.astype(BF).astype(F32)
    rest = value - high
    middle = rest.astype(BF).astype(F32)
    return [high, middle, rest - middle]


def eight(ref, group):
    return ref[pl.ds(pl.multiple_of(group * 8, 8), 8), :]


def couple_kernel(first_ref, nbr_ref, start_ref, len_ref, track_ref, low_ref, high_ref,
                  owner_ref, rank_ref, local_ref, node_ref, cap_ref, out_ref,
                  s_j, e_j, g_j, f_j, pick, shown, full_a, full_b,
                  left_a, left_b, right_a, right_b, acc):
    def fill(at, count, start, length, track):
        s_j[at:at + count, :] = start
        e_j[at:at + count, :] = start + length
        g_j[at:at + count, :] = jnp.exp(2.0 * track)
        f_j[at:at + count, :] = jnp.exp(-track)

    fill(8, ROWS, start_ref[...], len_ref[...], track_ref[...])
    fill(0, 8, low_ref[0:8, :], low_ref[8:16, :], low_ref[16:24, :])
    fill(8 + ROWS, 8, high_ref[0:8, :], high_ref[8:16, :], high_ref[16:24, :])
    row = lax.broadcasted_iota(jnp.int32, (SEG, 6 * SEG), 0)
    col = lax.broadcasted_iota(jnp.int32, (SEG, 6 * SEG), 1) >> 7
    array = jnp.where(row < 24, 0, jnp.where(row < 48, 1, jnp.where(row < 72, 2, 9)))
    pick[...] = jnp.where((row & 1) * 3 + array == col, 1.0, 0.0).astype(BF)
    pair_of = (lax.broadcasted_iota(jnp.int32, (SEG, SEG), 1) & 7) >> 1
    lane = lax.broadcasted_iota(jnp.int32, (8, SEG), 1)
    iota_o = iota_bf(ROWS, SEG)
    iota_r = iota_bf(CAPS, SEG)
    zero, one = jnp.zeros((), BF), jnp.ones((), BF)
    first = first_ref[0]

    def spread_columns(g, full):
        at = pl.ds(pl.multiple_of(8 + g * 8, 8), 8)
        pieces = split3(s_j[at, :]) + split3(e_j[at, :]) + split3(g_j[at, :])
        turned = jnp.concatenate(pieces + [jnp.zeros((SEG - 72, SEG), F32)], axis=0).T
        for pair in range(4):
            shown[pair * SEG:(pair + 1) * SEG, :] = jnp.where(pair_of == pair, turned, 0.0).astype(BF)
        full[...] = mm(shown[...], pick[...], NN)

    def pairs(g, j, full, sums):
        rows = []
        for k in range(4):
            near = jnp.clip(nbr_ref[g * 8 + j, k] - first + 8, 0, ROWS + 15)
            rows.append([
                jnp.broadcast_to(ref[pl.ds(near, 1), :], (8, SEG)) for ref in (s_j, e_j, g_j, f_j)
            ])
        base = (j & 1) * 3 * SEG
        for t in range(SEG // 8):
            part = slice((j >> 1) * SEG + 8 * t, (j >> 1) * SEG + 8 * t + 8)
            si = full[part, base:base + SEG]
            ei = full[part, base + SEG:base + 2 * SEG]
            gi = full[part, base + 2 * SEG:base + 3 * SEG]
            total = None
            for sj, ej, gj, fj in rows:
                common = jnp.maximum(jnp.minimum(ei, ej) - jnp.maximum(si, sj), 0.0)
                term = common * (jnp.minimum(gi, gj) * fj)
                total = term if total is None else total + term
            sums[t] = jnp.where(lane == j, jnp.sum(total, axis=1, keepdims=True), sums[t])

    def values_of(g):
        local, node = eight(local_ref, g), eight(node_ref, g)
        cap_hi, cap_lo = split(eight(cap_ref, g))
        res_hi, res_lo = split(SHEET * eight(len_ref, g))
        upper = (local >> 8) * NODES + node
        return [cap_hi, cap_lo, res_hi, res_lo,
                (upper * HALF).astype(F32), (local & (HALF - 1)).astype(F32)]

    def build(j, owner, rank, values, left, right):
        lanes = slice(j * SEG, (j + 1) * SEG)
        hit = iota_o == spread(owner[j:j + 1, :], ROWS)
        for p in range(6):
            value = spread(values[p][j:j + 1, :], ROWS)
            left[p * ROWS:(p + 1) * ROWS, lanes] = jnp.where(hit, value, zero)
        right[:, lanes] = jnp.where(iota_r == spread(rank[j:j + 1, :], CAPS), one, zero)

    def step(g, full, full_next, left, right, left_old, right_old):
        acc[...] += mm(left_old[...], right_old[...], NT)
        spread_columns(jnp.minimum(g + 1, ROWS // 8 - 1), full_next)
        last = jnp.maximum(g - 1, 0)
        owner = jnp.where(g > 0, eight(owner_ref, last).astype(F32), -1.0)
        rank, values = eight(rank_ref, last), values_of(last)
        sums = [jnp.zeros((8, SEG), F32)] * (SEG // 8)
        for j in range(8):
            build(j, owner, rank, values, left, right)
            pairs(g, j, full, sums)
        summed = jnp.concatenate(sums, axis=0).T[:8, :]
        at = pl.ds(pl.multiple_of(g * 8, 8), 8)
        scale = f_j[pl.ds(pl.multiple_of(8 + g * 8, 8), 8), :]
        cap_ref[at, :] = GROUND * len_ref[at, :] + COUPLE * scale * summed

    def two(h, carry):
        step(2 * h, full_a, full_b, left_a, right_a, left_b, right_b)
        step(2 * h + 1, full_b, full_a, left_b, right_b, left_a, right_a)
        return carry

    acc[...] = jnp.zeros_like(acc)
    cap_ref[0:8, :] = jnp.zeros((8, SEG), F32)
    left_b[...] = jnp.zeros_like(left_b)
    right_b[...] = jnp.zeros_like(right_b)
    spread_columns(0, full_a)
    lax.fori_loop(0, ROWS // 16, two, 0)
    last = ROWS // 8 - 1
    owner, rank, values = eight(owner_ref, last).astype(F32), eight(rank_ref, last), values_of(last)
    for j in range(8):
        build(j, owner, rank, values, left_a, right_a)
    acc[...] += mm(left_b[...], right_b[...], NT)
    acc[...] += mm(left_a[...], right_a[...], NT)
    for v in range(3):
        high = acc[2 * v * ROWS:(2 * v + 1) * ROWS, :]
        low = acc[(2 * v + 1) * ROWS:(2 * v + 2) * ROWS, :]
        out_ref[:, v * CAPS:(v + 1) * CAPS] = high + low


def owner_kernel(inbox_ref, pin_ref, load_ref, weight_ref, parent_ref, delay_ref, reply_ref,
                 upper_s, lower_s, pieces, left_a, left_b, right_a, right_b, found_a, found_b, acc):
    slot = inbox_ref[:, 2 * CAPS:].astype(jnp.int32)
    upper_s[...] = (slot >> 8).astype(F32)
    lower_s[...] = (slot & (HALF - 1)).astype(F32)
    for v in range(2):
        high, low = split(inbox_ref[:, v * CAPS:(v + 1) * CAPS])
        pieces[2 * v * ROWS:(2 * v + 1) * ROWS, :] = high
        pieces[(2 * v + 1) * ROWS:(2 * v + 2) * ROWS, :] = low
    acc[...] = jnp.zeros_like(acc)
    iota_u = iota_bf(64, CAPS)
    iota_l = iota_bf(HALF, CAPS)
    zero, one = jnp.zeros((), BF), jnp.ones((), BF)
    units = ROWS // 8

    def build_right(u, right):
        lower = eight(lower_s, u)
        for j in range(8):
            right[:, j * CAPS:(j + 1) * CAPS] = jnp.where(
                iota_l == spread(lower[j:j + 1, :], HALF), one, zero)

    def build_left(u, left):
        upper = eight(upper_s, u)
        values = [pieces[pl.ds(pl.multiple_of(p * ROWS + u * 8, 8), 8), :] for p in range(4)]
        for j in range(8):
            hit = iota_u == spread(upper[j:j + 1, :], 64)
            for p in range(4):
                left[p * 64:(p + 1) * 64, j * CAPS:(j + 1) * CAPS] = jnp.where(
                    hit, spread(values[p][j:j + 1, :], 64), zero)

    def collect(h, carry):
        for u, now, later in (
            (2 * h + 1, (left_a, right_a), (left_b, right_b)),
            (jnp.minimum(2 * h + 2, units - 1), (left_b, right_b), (left_a, right_a)),
        ):
            acc[...] += mm(now[0][...], now[1][...], NT)
            build_left(u, later[0])
            build_right(u, later[1])
        return carry

    build_left(0, left_a)
    build_right(0, right_a)
    lax.fori_loop(0, units // 2, collect, 0)

    def table(at):
        both = acc[at:at + 64, :] + acc[at + 64:at + 128, :]
        return jnp.concatenate([both[:NODES], both[NODES:]], axis=1)

    build_right(0, right_a)
    build_right(1, right_b)
    cap = load_ref[...] + table(0)
    res = pin_ref[...] + table(128)
    weight = weight_ref[...]
    iota8 = lax.broadcasted_iota(jnp.int32, (8, 2 * HALF), 0)
    tiles = NODES // 8
    cut = lambda a: [a[8 * t:8 * t + 8, :] for t in range(tiles)]
    sub, below, res = cut(cap), cut(weight), cut(res)
    for k in range(NODES - 1, 0, -1):
        t, r = divmod(k, 8)
        parent = jnp.broadcast_to(parent_ref[k:k + 1, :], iota8.shape)
        sub_k = jnp.broadcast_to(sub[t][r:r + 1, :], iota8.shape)
        below_k = jnp.broadcast_to(below[t][r:r + 1, :], iota8.shape)
        for a in range((k - 1) // 8 + 1):
            hit = parent == iota8 + 8 * a
            sub[a] = sub[a] + jnp.where(hit, sub_k, 0.0)
            below[a] = below[a] + jnp.where(hit, below_k, 0.0)
    step_d = [res[t] * sub[t] for t in range(tiles)]
    step_g = [res[t] * below[t] for t in range(tiles)]
    down_d, down_g = list(step_d), list(step_g)
    for k in range(1, NODES):
        t, r = divmod(k, 8)
        parent = jnp.broadcast_to(parent_ref[k:k + 1, :], iota8.shape)
        from_d = from_g = None
        for a in range((k - 1) // 8 + 1):
            hit = parent == iota8 + 8 * a
            d, g = jnp.where(hit, down_d[a], 0.0), jnp.where(hit, down_g[a], 0.0)
            from_d = d if from_d is None else from_d + d
            from_g = g if from_g is None else from_g + g
        here = iota8 == r
        down_d[t] = jnp.where(here, step_d[t] + jnp.sum(from_d, axis=0, keepdims=True), down_d[t])
        down_g[t] = jnp.where(here, step_g[t] + jnp.sum(from_g, axis=0, keepdims=True), down_g[t])
    delay_ref[...] = jnp.concatenate(down_d, axis=0)
    sens = jnp.concatenate(
        [SHEET * (below[t] * sub[t]) + GROUND * down_g[t] for t in range(tiles)], axis=0)
    high, low = split(sens)
    left_a[0:ROWS, 0:HALF] = jnp.concatenate(
        [high[:, :HALF], high[:, HALF:], low[:, :HALF], low[:, HALF:]], axis=0).astype(BF)
    iota_uf = lax.broadcasted_iota(jnp.int32, (64, CAPS), 0).astype(F32)

    def look_up(right, found):
        found[...] = mm(left_a[0:ROWS, 0:HALF], right[...], NN)

    def answer(u, found):
        upper = eight(upper_s, u)
        rows = []
        for j in range(8):
            both = found[:, j * CAPS:(j + 1) * CAPS]
            kept = jnp.where(iota_uf == upper[j:j + 1, :], both[:64] + both[64:], 0.0)
            rows.append(jnp.sum(kept, axis=0, keepdims=True))
        reply_ref[pl.ds(pl.multiple_of(u * 8, 8), 8), :] = jnp.concatenate(rows, axis=0)

    def answers(h, carry):
        look_up(right_b, found_b)
        answer(2 * h, found_a)
        build_right(jnp.minimum(2 * h + 2, units - 1), right_a)
        look_up(right_a, found_a)
        answer(2 * h + 1, found_b)
        build_right(jnp.minimum(2 * h + 3, units - 1), right_b)
        return carry

    look_up(right_a, found_a)
    lax.fori_loop(0, units // 2, answers, 0)


def final_kernel(returned_ref, owner_ref, rank_ref, out_ref, picks, ones_a, ones_b, found_a, found_b):
    high, low = split(returned_ref[...])
    picks[...] = jnp.concatenate([high, low], axis=0).astype(BF)
    iota_r = iota_bf(CAPS, 2 * SEG)
    iota_o = lax.broadcasted_iota(jnp.int32, (ROWS, 2 * SEG), 0)
    zero, one = jnp.zeros((), BF), jnp.ones((), BF)
    units = ROWS // 8

    def pair(rows, j):
        return jnp.concatenate([rows[2 * j:2 * j + 1, :], rows[2 * j + 1:2 * j + 2, :]], axis=1)

    def build(u, ones):
        rank = eight(rank_ref, u)
        for j in range(4):
            ones[:, j * 2 * SEG:(j + 1) * 2 * SEG] = jnp.where(
                iota_r == spread(pair(rank, j), CAPS), one, zero)

    def look_up(ones, found):
        found[...] = mm(picks[...], ones[...], NN)

    def answer(u, found):
        owner = eight(owner_ref, u)
        rows = []
        for j in range(4):
            both = found[:, j * 2 * SEG:(j + 1) * 2 * SEG]
            kept = jnp.where(iota_o == pair(owner, j), both[:ROWS] + both[ROWS:], 0.0)
            row = jnp.sum(kept, axis=0, keepdims=True)
            rows += [row[:, :SEG], row[:, SEG:]]
        out_ref[pl.ds(pl.multiple_of(u * 8, 8), 8), :] = jnp.concatenate(rows, axis=0)

    def two(h, carry):
        look_up(ones_b, found_b)
        answer(2 * h, found_a)
        build(jnp.minimum(2 * h + 2, units - 1), ones_a)
        look_up(ones_a, found_a)
        answer(2 * h + 1, found_b)
        build(jnp.minimum(2 * h + 3, units - 1), ones_b)
        return carry

    build(0, ones_a)
    build(1, ones_b)
    look_up(ones_a, found_a)
    lax.fori_loop(0, units // 2, two, 0)


def call(kernel, name, shapes, in_specs, scratch=()):
    vmem = pl.BlockSpec(memory_space=pltpu.VMEM)
    smem = pl.BlockSpec(memory_space=pltpu.SMEM)
    specs = [smem if c == "s" else vmem for c in in_specs]
    outs = [jax.ShapeDtypeStruct(shape, F32) for shape in shapes]
    single = len(outs) == 1
    return pl.pallas_call(
        kernel,
        out_shape=outs[0] if single else outs,
        in_specs=specs,
        out_specs=vmem if single else [vmem] * len(outs),
        scratch_shapes=[pltpu.VMEM(shape, dtype) for shape, dtype in scratch],
        compiler_params=pltpu.CompilerParams(vmem_limit_bytes=VMEM_LIMIT),
        name=name,
    )


def exchange(box):
    return lax.all_to_all(box, AXES, split_axis=0, concat_axis=0, tiled=True)


def body(seg_start, seg_len, seg_track, seg_nbr, seg_owner, seg_local, seg_node,
         pin_res, load_cap, crit_weight, net_parent):
    devices = lax.axis_size(AXES)
    forward = [(i, i + 1) for i in range(devices - 1)]
    backward = [(i + 1, i) for i in range(devices - 1)]
    feats = (seg_start, seg_len, seg_track)
    low = lax.ppermute(jnp.concatenate([f[-8:] for f in feats], axis=0), AXES, forward)
    high = lax.ppermute(jnp.concatenate([f[:8] for f in feats], axis=0), AXES, backward)
    owner = seg_owner.reshape(ROWS, SEG)
    square, flat = (ROWS, SEG), (ROWS, CAPS)
    rank = call(rank_kernel, "rank", [square], "v")(owner)
    first = (lax.axis_index(AXES) * ROWS).astype(jnp.int32).reshape(1)
    wide = (ROWS + 16, SEG)
    seg_cap, outbox = call(
        couple_kernel, "couple", [square, (ROWS, 3 * CAPS)], "ssvvvvvvvvv",
        [(wide, F32)] * 4 + [((SEG, 6 * SEG), BF), ((4 * SEG, SEG), BF)]
        + [((4 * SEG, 6 * SEG), F32)] * 2 + [((6 * ROWS, 8 * SEG), BF)] * 2
        + [((CAPS, 8 * SEG), BF)] * 2 + [((6 * ROWS, CAPS), F32)],
    )(first, seg_nbr, seg_start, seg_len, seg_track, low, high, owner, rank, seg_local, seg_node)
    inbox = exchange(outbox)
    delay, reply = call(
        owner_kernel, "owner", [(NODES, 2 * HALF), flat], "vvvvv",
        [(flat, F32), (flat, F32), ((4 * ROWS, CAPS), F32)] + [((CAPS, 8 * CAPS), BF)] * 4
        + [((ROWS, 8 * CAPS), F32)] * 2 + [((CAPS, HALF), F32)],
    )(inbox, pin_res, load_cap, crit_weight, net_parent)
    returned = exchange(reply)
    seg_sens = call(
        final_kernel, "final", [square], "vvv",
        [((2 * ROWS, CAPS), BF)] + [((CAPS, 8 * SEG), BF)] * 2 + [((2 * ROWS, 8 * SEG), F32)] * 2,
    )(returned, owner, rank)
    return seg_cap, delay, seg_sens


def solution(mesh):
    rows, nets = P(AXES, None), P(None, AXES)
    placed = (rows, rows, rows, rows, P(AXES, None, None), rows, rows, nets, nets, nets, nets)
    return jax.shard_map(body, mesh=mesh, in_specs=placed, out_specs=(rows, nets, rows), check_vma=False)
```

```python
import jax
import jax.numpy as jnp
from jax import lax
from jax.experimental import pallas as pl
from jax.experimental.pallas import tpu as pltpu
from jax.sharding import PartitionSpec as P

RIM = 4
GROUND = 0.2
COUPLE = 0.005
SHEET = 0.02
AXES = ("tile", "net")
BF = jnp.bfloat16
F32 = jnp.float32

ROWS = 128
SEG = 128
CAPS = 256
NODES = 32
HALF = 256
VMEM_LIMIT = 48 * 1024 * 1024

RANK_ROWS = 64
COUPLE_STEPS = 2
OWNER_UNITS = 8
FINAL_UNITS = 16

NT = (((1,), (1,)), ((), ()))
NN = (((1,), (0,)), ((), ()))


def mm(left, right, dims):
    return lax.dot_general(left, right, dims, preferred_element_type=F32)


def iota_bf(rows, cols):
    return lax.broadcasted_iota(jnp.int32, (rows, cols), 0).astype(F32).astype(BF)


def spread(row, rows):
    sixteen = jnp.broadcast_to(row, (16, row.shape[1])).astype(BF)
    return jnp.concatenate([sixteen] * (rows // 16), axis=0)


def split(value):
    high = value.astype(BF).astype(F32)
    return high, (value - high).astype(BF).astype(F32)


def repeat(count, together, step):
    def several(h, carry):
        for q in range(together):
            step(h * together + q)
        return carry

    if count == together:
        several(0, 0)
    else:
        lax.fori_loop(0, count // together, several, 0)


def rank_kernel(owner_ref, rank_ref):
    iota = lax.broadcasted_iota(jnp.int32, (ROWS, SEG), 0)
    r0 = lax.broadcasted_iota(jnp.int32, (SEG, 2 * SEG), 0)
    c0 = lax.broadcasted_iota(jnp.int32, (SEG, 2 * SEG), 1)
    upper = jnp.where((r0 <= c0), 1.0, 0.0).astype(BF)

    def step(g, before):
        for j in range(RANK_ROWS):
            b = g * RANK_ROWS + j
            hit = iota == owner_ref[pl.ds(b, 1), :]
            ones = jnp.where(hit, 1.0, 0.0).astype(BF)
            sums = mm(ones, upper, NN)
            placed = jnp.where(hit, sums[:, :SEG] + before, 0.0)
            rank_ref[pl.ds(b, 1), :] = jnp.sum(placed, axis=0, keepdims=True) - 1.0
            before = before + sums[:, SEG:]
        return before

    lax.fori_loop(0, ROWS // RANK_ROWS, step, jnp.zeros((ROWS, SEG), F32))


def split3(value):
    high = value.astype(BF).astype(F32)
    rest = value - high
    middle = rest.astype(BF).astype(F32)
    return [high, middle, rest - middle]


def eight(ref, group):
    return ref[pl.ds(pl.multiple_of(group * 8, 8), 8), :]


def couple_kernel(first_ref, nbr_ref, start_ref, len_ref, track_ref, low_ref, high_ref,
                  owner_ref, rank_ref, local_ref, node_ref, cap_ref, out_ref,
                  s_j, e_j, g_j, f_j, pick, full_a, full_b, acc):
    def fill(at, count, start, length, track):
        s_j[at:at + count, :] = start
        e_j[at:at + count, :] = start + length
        g_j[at:at + count, :] = jnp.exp(2.0 * track)
        f_j[at:at + count, :] = jnp.exp(-track)

    fill(8, ROWS, start_ref[...], len_ref[...], track_ref[...])
    fill(0, 8, low_ref[0:8, :], low_ref[8:16, :], low_ref[16:24, :])
    fill(8 + ROWS, 8, high_ref[0:8, :], high_ref[8:16, :], high_ref[16:24, :])
    row = lax.broadcasted_iota(jnp.int32, (SEG, 6 * SEG), 0)
    col = lax.broadcasted_iota(jnp.int32, (SEG, 6 * SEG), 1) >> 7
    array = jnp.where(row < 24, 0, jnp.where(row < 48, 1, jnp.where(row < 72, 2, 9)))
    pick[...] = jnp.where((row & 1) * 3 + array == col, 1.0, 0.0).astype(BF)
    pair_of = (lax.broadcasted_iota(jnp.int32, (SEG, SEG), 1) & 7) >> 1
    lane = lax.broadcasted_iota(jnp.int32, (8, SEG), 1)
    iota_o = iota_bf(ROWS, SEG)
    iota_r = iota_bf(CAPS, SEG)
    zero, one = jnp.zeros((), BF), jnp.ones((), BF)
    first = first_ref[0]

    def turn(g, full):
        at = pl.ds(pl.multiple_of(8 + g * 8, 8), 8)
        pieces = split3(s_j[at, :]) + split3(e_j[at, :]) + split3(g_j[at, :])
        turned = jnp.concatenate(pieces + [jnp.zeros((SEG - 72, SEG), F32)], axis=0).T
        full[...] = turned

    def spread_pair(pair, full):
        part = jnp.where(pair_of == pair, full[...], 0.0).astype(BF)
        return mm(part, pick[...], NN)

    def pairs(g, j, full, sums):
        rows = []
        for k in range(4):
            near = jnp.clip(nbr_ref[g * 8 + j, k] - first + 8, 0, ROWS + 15)
            rows.append([
                jnp.broadcast_to(ref[pl.ds(near, 1), :], (8, SEG)) for ref in (s_j, e_j, g_j, f_j)
            ])
        base = (j & 1) * 3 * SEG
        for t in range(SEG // 8):
            part = slice(8 * t, 8 * t + 8)
            si = full[part, base:base + SEG]
            ei = full[part, base + SEG:base + 2 * SEG]
            gi = full[part, base + 2 * SEG:base + 3 * SEG]
            total = None
            for sj, ej, gj, fj in rows:
                common = jnp.maximum(jnp.minimum(ei, ej) - jnp.maximum(si, sj), 0.0)
                term = common * (jnp.minimum(gi, gj) * fj)
                total = term if total is None else total + term
            sums[t] = jnp.where(lane == j, jnp.sum(total, axis=1, keepdims=True), sums[t])

    def values_of(g):
        local, node = eight(local_ref, g), eight(node_ref, g)
        cap_hi, cap_lo = split(eight(cap_ref, g))
        res_hi, res_lo = split(SHEET * eight(len_ref, g))
        slot = ((local >> 8) * NODES + node) * HALF + (local & (HALF - 1))
        power = jnp.exp2(((slot >> 7) - 63).astype(F32))
        return [cap_hi, cap_lo, res_hi, res_lo, power * (1.0 + (slot & 127).astype(F32) * (1.0 / 128))]

    def send(j0, owner, rank, values):
        cols = []
        rows = []
        for j in range(j0, j0 + 4):
            hit = iota_o == spread(owner[j:j + 1, :], ROWS)
            cols.append(jnp.concatenate(
                [jnp.where(hit, spread(v[j:j + 1, :], ROWS), zero) for v in values], axis=0))
            rows.append(jnp.where(iota_r == spread(rank[j:j + 1, :], CAPS), one, zero))
        acc[...] += mm(jnp.concatenate(cols, axis=1), jnp.concatenate(rows, axis=1), NT)

    def step(g, full, full_next):
        turn(jnp.minimum(g + 1, ROWS // 8 - 1), full_next)
        last = jnp.maximum(g - 1, 0)
        owner = jnp.where(g > 0, eight(owner_ref, last).astype(F32), -1.0)
        rank, values = eight(rank_ref, last), values_of(last)
        sums = [jnp.zeros((8, SEG), F32)] * (SEG // 8)
        for j in range(8):
            if j % 4 == 0:
                send(j, owner, rank, values)
            if j % 2 == 0:
                wide = spread_pair(j // 2, full)
            pairs(g, j, wide, sums)
        summed = jnp.concatenate(sums, axis=0).T[:8, :]
        at = pl.ds(pl.multiple_of(g * 8, 8), 8)
        scale = f_j[pl.ds(pl.multiple_of(8 + g * 8, 8), 8), :]
        cap_ref[at, :] = GROUND * len_ref[at, :] + COUPLE * scale * summed

    def several(h, carry):
        for q in range(0, COUPLE_STEPS, 2):
            step(COUPLE_STEPS * h + q, full_a, full_b)
            step(COUPLE_STEPS * h + q + 1, full_b, full_a)
        return carry

    acc[...] = jnp.zeros_like(acc)
    cap_ref[0:8, :] = jnp.zeros((8, SEG), F32)
    turn(0, full_a)
    lax.fori_loop(0, ROWS // 8 // COUPLE_STEPS, several, 0)
    last = ROWS // 8 - 1
    owner, rank, values = eight(owner_ref, last).astype(F32), eight(rank_ref, last), values_of(last)
    for j in range(0, 8, 4):
        send(j, owner, rank, values)
    for v in range(2):
        high = acc[2 * v * ROWS:(2 * v + 1) * ROWS, :]
        low = acc[(2 * v + 1) * ROWS:(2 * v + 2) * ROWS, :]
        out_ref[:, v * CAPS:(v + 1) * CAPS] = high + low
    coded = jnp.maximum(acc[4 * ROWS:5 * ROWS, :], 2.0 ** -63)
    power = jnp.floor(jnp.log2(coded) + 63.002)
    fraction = jnp.floor((coded * jnp.exp2(63.0 - power) - 1.0) * 128.0 + 0.5)
    out_ref[:, 2 * CAPS:] = power * 128.0 + fraction


def owner_kernel(inbox_ref, pin_ref, load_ref, weight_ref, parent_ref, delay_ref, reply_ref,
                 upper_s, lower_s, pieces, picks, acc):
    slot = inbox_ref[:, 2 * CAPS:].astype(jnp.int32)
    upper_s[...] = (slot >> 8).astype(F32)
    lower_s[...] = (slot & (HALF - 1)).astype(F32)
    for v in range(2):
        high, low = split(inbox_ref[:, v * CAPS:(v + 1) * CAPS])
        pieces[2 * v * ROWS:(2 * v + 1) * ROWS, :] = high
        pieces[(2 * v + 1) * ROWS:(2 * v + 2) * ROWS, :] = low
    acc[...] = jnp.zeros_like(acc)
    iota_u = iota_bf(64, CAPS)
    iota_l = iota_bf(HALF, CAPS)
    zero, one = jnp.zeros((), BF), jnp.ones((), BF)
    units = ROWS // 8

    def lower_ones(lower, j):
        return jnp.where(iota_l == spread(lower[j:j + 1, :], HALF), one, zero)

    def collect(u):
        upper, lower = eight(upper_s, u), eight(lower_s, u)
        values = [pieces[pl.ds(pl.multiple_of(p * ROWS + u * 8, 8), 8), :] for p in range(4)]
        for j0 in (0, 4):
            left, right = [], []
            for j in range(j0, j0 + 4):
                hit = iota_u == spread(upper[j:j + 1, :], 64)
                left.append(jnp.concatenate(
                    [jnp.where(hit, spread(v[j:j + 1, :], 64), zero) for v in values], axis=0))
                right.append(lower_ones(lower, j))
            acc[...] += mm(jnp.concatenate(left, axis=1), jnp.concatenate(right, axis=1), NT)

    repeat(units, OWNER_UNITS, collect)

    def table(at):
        both = acc[at:at + 64, :] + acc[at + 64:at + 128, :]
        return jnp.concatenate([both[:NODES], both[NODES:]], axis=1)

    cap = load_ref[...] + table(0)
    res = pin_ref[...] + table(128)
    weight = weight_ref[...]
    iota8 = lax.broadcasted_iota(jnp.int32, (8, 2 * HALF), 0)
    tiles = NODES // 8
    cut = lambda a: [a[8 * t:8 * t + 8, :] for t in range(tiles)]
    sub, below, res = cut(cap), cut(weight), cut(res)
    for k in range(NODES - 1, 0, -1):
        t, r = divmod(k, 8)
        parent = jnp.broadcast_to(parent_ref[k:k + 1, :], iota8.shape)
        sub_k = jnp.broadcast_to(sub[t][r:r + 1, :], iota8.shape)
        below_k = jnp.broadcast_to(below[t][r:r + 1, :], iota8.shape)
        for a in range((k - 1) // 8 + 1):
            hit = parent == iota8 + 8 * a
            sub[a] = sub[a] + jnp.where(hit, sub_k, 0.0)
            below[a] = below[a] + jnp.where(hit, below_k, 0.0)
    step_d = [res[t] * sub[t] for t in range(tiles)]
    step_g = [res[t] * below[t] for t in range(tiles)]
    down_d, down_g = list(step_d), list(step_g)
    for k in range(1, NODES):
        t, r = divmod(k, 8)
        parent = jnp.broadcast_to(parent_ref[k:k + 1, :], iota8.shape)
        from_d = from_g = None
        for a in range((k - 1) // 8 + 1):
            hit = parent == iota8 + 8 * a
            d, g = jnp.where(hit, down_d[a], 0.0), jnp.where(hit, down_g[a], 0.0)
            from_d = d if from_d is None else from_d + d
            from_g = g if from_g is None else from_g + g
        here = iota8 == r
        down_d[t] = jnp.where(here, step_d[t] + jnp.sum(from_d, axis=0, keepdims=True), down_d[t])
        down_g[t] = jnp.where(here, step_g[t] + jnp.sum(from_g, axis=0, keepdims=True), down_g[t])
    delay_ref[...] = jnp.concatenate(down_d, axis=0)
    sens = jnp.concatenate(
        [SHEET * (below[t] * sub[t]) + GROUND * down_g[t] for t in range(tiles)], axis=0)
    high, low = split(sens)
    picks[...] = jnp.concatenate(
        [high[:, :HALF], high[:, HALF:], low[:, :HALF], low[:, HALF:]], axis=0).astype(BF)
    iota_uf = lax.broadcasted_iota(jnp.int32, (64, CAPS), 0).astype(F32)

    def answer(u):
        upper, lower = eight(upper_s, u), eight(lower_s, u)
        rows = []
        for j in range(8):
            both = mm(picks[...], lower_ones(lower, j), NN)
            kept = jnp.where(iota_uf == upper[j:j + 1, :], both[:64] + both[64:], 0.0)
            rows.append(jnp.sum(kept, axis=0, keepdims=True))
        reply_ref[pl.ds(pl.multiple_of(u * 8, 8), 8), :] = jnp.concatenate(rows, axis=0)

    repeat(units, OWNER_UNITS, answer)


def final_kernel(returned_ref, owner_ref, rank_ref, out_ref, picks):
    high, low = split(returned_ref[...])
    picks[...] = jnp.concatenate([high, low], axis=0).astype(BF)
    iota_r = iota_bf(CAPS, 2 * SEG)
    iota_o = lax.broadcasted_iota(jnp.int32, (ROWS, 2 * SEG), 0)
    zero, one = jnp.zeros((), BF), jnp.ones((), BF)

    def pair(rows, j):
        return jnp.concatenate([rows[2 * j:2 * j + 1, :], rows[2 * j + 1:2 * j + 2, :]], axis=1)

    def answer(u):
        rank, owner = eight(rank_ref, u), eight(owner_ref, u)
        rows = []
        for j in range(4):
            ones = jnp.where(iota_r == spread(pair(rank, j), CAPS), one, zero)
            both = mm(picks[...], ones, NN)
            kept = jnp.where(iota_o == pair(owner, j), both[:ROWS] + both[ROWS:], 0.0)
            row = jnp.sum(kept, axis=0, keepdims=True)
            rows += [row[:, :SEG], row[:, SEG:]]
        out_ref[pl.ds(pl.multiple_of(u * 8, 8), 8), :] = jnp.concatenate(rows, axis=0)

    repeat(ROWS // 8, FINAL_UNITS, answer)


def call(kernel, name, shapes, in_specs, scratch=()):
    vmem = pl.BlockSpec(memory_space=pltpu.VMEM)
    smem = pl.BlockSpec(memory_space=pltpu.SMEM)
    specs = [smem if c == "s" else vmem for c in in_specs]
    outs = [jax.ShapeDtypeStruct(shape, F32) for shape in shapes]
    single = len(outs) == 1
    return pl.pallas_call(
        kernel,
        out_shape=outs[0] if single else outs,
        in_specs=specs,
        out_specs=vmem if single else [vmem] * len(outs),
        scratch_shapes=[pltpu.VMEM(shape, dtype) for shape, dtype in scratch],
        compiler_params=pltpu.CompilerParams(vmem_limit_bytes=VMEM_LIMIT),
        name=name,
    )


def exchange(box):
    return lax.all_to_all(box, AXES, split_axis=0, concat_axis=0, tiled=True)


def body(seg_start, seg_len, seg_track, seg_nbr, seg_owner, seg_local, seg_node,
         pin_res, load_cap, crit_weight, net_parent):
    devices = lax.axis_size(AXES)
    forward = [(i, i + 1) for i in range(devices - 1)]
    backward = [(i + 1, i) for i in range(devices - 1)]
    feats = (seg_start, seg_len, seg_track)
    low = lax.ppermute(jnp.concatenate([f[-8:] for f in feats], axis=0), AXES, forward)
    high = lax.ppermute(jnp.concatenate([f[:8] for f in feats], axis=0), AXES, backward)
    owner = seg_owner.reshape(ROWS, SEG)
    square, flat = (ROWS, SEG), (ROWS, CAPS)
    rank = call(rank_kernel, "rank", [square], "v")(owner)
    first = (lax.axis_index(AXES) * ROWS).astype(jnp.int32).reshape(1)
    wide = (ROWS + 16, SEG)
    seg_cap, outbox = call(
        couple_kernel, "couple", [square, (ROWS, 3 * CAPS)], "ssvvvvvvvvv",
        [(wide, F32)] * 4 + [((SEG, 6 * SEG), BF)] + [(square, F32)] * 2 + [((5 * ROWS, CAPS), F32)],
    )(first, seg_nbr, seg_start, seg_len, seg_track, low, high, owner, rank, seg_local, seg_node)
    inbox = exchange(outbox)
    delay, reply = call(
        owner_kernel, "owner", [(NODES, 2 * HALF), flat], "vvvvv",
        [(flat, F32), (flat, F32), ((4 * ROWS, CAPS), F32), ((ROWS, HALF), BF), ((CAPS, HALF), F32)],
    )(inbox, pin_res, load_cap, crit_weight, net_parent)
    returned = exchange(reply)
    seg_sens = call(
        final_kernel, "final", [square], "vvv",
        [((2 * ROWS, CAPS), BF)],
    )(returned, owner, rank)
    return seg_cap, delay, seg_sens


def solution(mesh):
    rows, nets = P(AXES, None), P(None, AXES)
    placed = (rows, rows, rows, rows, P(AXES, None, None), rows, rows, nets, nets, nets, nets)
    return jax.shard_map(body, mesh=mesh, in_specs=placed, out_specs=(rows, nets, rows), check_vma=False)
```

```python
import jax
import jax.numpy as jnp
from jax import lax
from jax.experimental import pallas as pl
from jax.experimental.pallas import tpu as pltpu
from jax.sharding import PartitionSpec as P

RIM = 4
GROUND = 0.2
COUPLE = 0.005
SHEET = 0.02
AXES = ("tile", "net")
BF = jnp.bfloat16
F32 = jnp.float32

ROWS = 128
SEG = 128
CAPS = 256
NODES = 32
HALF = 256
VMEM_LIMIT = 24 * 1024 * 1024

RANK_ROWS = 64
COUPLE_STEPS = 2
OWNER_UNITS = 8
FINAL_UNITS = 16

NT = (((1,), (1,)), ((), ()))
NN = (((1,), (0,)), ((), ()))


def mm(left, right, dims):
    return lax.dot_general(left, right, dims, preferred_element_type=F32)


def iota_bf(rows, cols):
    return lax.broadcasted_iota(jnp.int32, (rows, cols), 0).astype(F32).astype(BF)


def spread(row, rows):
    sixteen = jnp.broadcast_to(row, (16, row.shape[1])).astype(BF)
    return jnp.concatenate([sixteen] * (rows // 16), axis=0)


def split(value):
    high = value.astype(BF).astype(F32)
    return high, (value - high).astype(BF).astype(F32)


def repeat(count, together, step):
    def several(h, carry):
        for q in range(together):
            step(h * together + q)
        return carry

    if count == together:
        several(0, 0)
    else:
        lax.fori_loop(0, count // together, several, 0)


def even_device(first_ref):
    return ((first_ref[0] // ROWS) & 1) == 0


def copy_all(pairs, sems):
    copies = [pltpu.make_async_copy(source, target, sems.at[n]) for n, (source, target) in enumerate(pairs)]
    for copy in copies:
        copy.start()
    return copies


def edge_kernel(first_ref, start_hbm, len_hbm, track_hbm, near_ref, far_ref, sems):
    even = even_device(first_ref)
    high = pl.multiple_of(jnp.where(even, ROWS - 8, 0), 8)
    low = pl.multiple_of(jnp.where(even, 0, ROWS - 8), 8)
    pairs = []
    for n, source in enumerate((start_hbm, len_hbm, track_hbm)):
        pairs.append((source.at[pl.ds(low, 8), :], far_ref.at[8 * n:8 * n + 8, :]))
        pairs.append((source.at[pl.ds(high, 8), :], near_ref.at[8 * n:8 * n + 8, :]))
    for copy in copy_all(pairs, sems):
        copy.wait()


def rank_kernel(owner_ref, rank_ref):
    iota = lax.broadcasted_iota(jnp.int32, (ROWS, SEG), 0)
    r0 = lax.broadcasted_iota(jnp.int32, (SEG, 2 * SEG), 0)
    c0 = lax.broadcasted_iota(jnp.int32, (SEG, 2 * SEG), 1)
    upper = jnp.where((r0 <= c0), 1.0, 0.0).astype(BF)

    def step(g, before):
        for j in range(RANK_ROWS):
            b = g * RANK_ROWS + j
            hit = iota == owner_ref[pl.ds(b, 1), :]
            ones = jnp.where(hit, 1.0, 0.0).astype(BF)
            sums = mm(ones, upper, NN)
            placed = jnp.where(hit, sums[:, :SEG] + before, 0.0)
            rank_ref[pl.ds(b, 1), :] = jnp.sum(placed, axis=0, keepdims=True) - 1.0
            before = before + sums[:, SEG:]
        return before

    lax.fori_loop(0, ROWS // RANK_ROWS, step, jnp.zeros((ROWS, SEG), F32))


def split3(value):
    high = value.astype(BF).astype(F32)
    rest = value - high
    middle = rest.astype(BF).astype(F32)
    return [high, middle, rest - middle]


def eight(ref, group):
    return ref[pl.ds(pl.multiple_of(group * 8, 8), 8), :]


def lines(value, half, width):
    return pl.ds(2 * value + half, ROWS, stride=width)


def place(ref, value, array):
    for half in (0, 1):
        ref[lines(value, half, 6), :] = array[:, half * SEG:(half + 1) * SEG]


def take(ref, value, width):
    return jnp.concatenate([ref[lines(value, half, width), :] for half in (0, 1)], axis=1)


def couple_kernel(first_ref, nbr_ref, start_ref, len_ref, track_ref, near_ref, far_ref,
                  owner_ref, rank_ref, local_ref, node_ref, cap_ref, out_ref,
                  s_j, e_j, g_j, f_j, pick, full_a, full_b, acc):
    def fill(at, count, start, length, track):
        s_j[at:at + count, :] = start
        e_j[at:at + count, :] = start + length
        g_j[at:at + count, :] = jnp.exp(2.0 * track)
        f_j[at:at + count, :] = jnp.exp(-track)

    fill(8, ROWS, start_ref[...], len_ref[...], track_ref[...])
    even, near, far = even_device(first_ref), near_ref[...], far_ref[...]
    low, high = jnp.where(even, far, near), jnp.where(even, near, far)
    fill(0, 8, low[0:8, :], low[8:16, :], low[16:24, :])
    fill(8 + ROWS, 8, high[0:8, :], high[8:16, :], high[16:24, :])
    row = lax.broadcasted_iota(jnp.int32, (SEG, 6 * SEG), 0)
    col = lax.broadcasted_iota(jnp.int32, (SEG, 6 * SEG), 1) >> 7
    array = jnp.where(row < 24, 0, jnp.where(row < 48, 1, jnp.where(row < 72, 2, 9)))
    pick[...] = jnp.where((row & 1) * 3 + array == col, 1.0, 0.0).astype(BF)
    pair_of = (lax.broadcasted_iota(jnp.int32, (SEG, SEG), 1) & 7) >> 1
    lane = lax.broadcasted_iota(jnp.int32, (8, SEG), 1)
    iota_o = iota_bf(ROWS, SEG)
    iota_r = iota_bf(CAPS, SEG)
    zero, one = jnp.zeros((), BF), jnp.ones((), BF)
    first = first_ref[0]

    def turn(g, full):
        at = pl.ds(pl.multiple_of(8 + g * 8, 8), 8)
        pieces = split3(s_j[at, :]) + split3(e_j[at, :]) + split3(g_j[at, :])
        turned = jnp.concatenate(pieces + [jnp.zeros((SEG - 72, SEG), F32)], axis=0).T
        full[...] = turned

    def spread_pair(pair, full):
        part = jnp.where(pair_of == pair, full[...], 0.0).astype(BF)
        return mm(part, pick[...], NN)

    def pairs(g, j, full, sums):
        rows = []
        for k in range(4):
            near = jnp.clip(nbr_ref[k, g * 8 + j] - first + 8, 0, ROWS + 15)
            rows.append([
                jnp.broadcast_to(ref[pl.ds(near, 1), :], (8, SEG)) for ref in (s_j, e_j, g_j, f_j)
            ])
        base = (j & 1) * 3 * SEG
        for t in range(SEG // 8):
            part = slice(8 * t, 8 * t + 8)
            si = full[part, base:base + SEG]
            ei = full[part, base + SEG:base + 2 * SEG]
            gi = full[part, base + 2 * SEG:base + 3 * SEG]
            total = None
            for sj, ej, gj, fj in rows:
                common = jnp.maximum(jnp.minimum(ei, ej) - jnp.maximum(si, sj), 0.0)
                term = common * (jnp.minimum(gi, gj) * fj)
                total = term if total is None else total + term
            sums[t] = jnp.where(lane == j, jnp.sum(total, axis=1, keepdims=True), sums[t])

    def values_of(g):
        local, node = eight(local_ref, g), eight(node_ref, g)
        cap_hi, cap_lo = split(eight(cap_ref, g))
        res_hi, res_lo = split(SHEET * eight(len_ref, g))
        slot = ((local >> 8) * NODES + node) * HALF + (local & (HALF - 1))
        power = jnp.exp2(((slot >> 7) - 63).astype(F32))
        return [cap_hi, cap_lo, res_hi, res_lo, power * (1.0 + (slot & 127).astype(F32) * (1.0 / 128))]

    def send(j0, owner, rank, values):
        cols = []
        rows = []
        for j in range(j0, j0 + 4):
            hit = iota_o == spread(owner[j:j + 1, :], ROWS)
            cols.append(jnp.concatenate(
                [jnp.where(hit, spread(v[j:j + 1, :], ROWS), zero) for v in values], axis=0))
            rows.append(jnp.where(iota_r == spread(rank[j:j + 1, :], CAPS), one, zero))
        acc[...] += mm(jnp.concatenate(cols, axis=1), jnp.concatenate(rows, axis=1), NT)

    def step(g, full, full_next):
        turn(jnp.minimum(g + 1, ROWS // 8 - 1), full_next)
        last = jnp.maximum(g - 1, 0)
        owner = jnp.where(g > 0, eight(owner_ref, last).astype(F32), -1.0)
        rank, values = eight(rank_ref, last), values_of(last)
        sums = [jnp.zeros((8, SEG), F32)] * (SEG // 8)
        for j in range(8):
            if j % 4 == 0:
                send(j, owner, rank, values)
            if j % 2 == 0:
                wide = spread_pair(j // 2, full)
            pairs(g, j, wide, sums)
        summed = jnp.concatenate(sums, axis=0).T[:8, :]
        at = pl.ds(pl.multiple_of(g * 8, 8), 8)
        scale = f_j[pl.ds(pl.multiple_of(8 + g * 8, 8), 8), :]
        cap_ref[at, :] = GROUND * len_ref[at, :] + COUPLE * scale * summed

    def several(h, carry):
        for q in range(0, COUPLE_STEPS, 2):
            step(COUPLE_STEPS * h + q, full_a, full_b)
            step(COUPLE_STEPS * h + q + 1, full_b, full_a)
        return carry

    acc[...] = jnp.zeros_like(acc)
    cap_ref[0:8, :] = jnp.zeros((8, SEG), F32)
    turn(0, full_a)
    lax.fori_loop(0, ROWS // 8 // COUPLE_STEPS, several, 0)
    last = ROWS // 8 - 1
    owner, rank, values = eight(owner_ref, last).astype(F32), eight(rank_ref, last), values_of(last)
    for j in range(0, 8, 4):
        send(j, owner, rank, values)
    for v in range(2):
        high = acc[2 * v * ROWS:(2 * v + 1) * ROWS, :]
        low = acc[(2 * v + 1) * ROWS:(2 * v + 2) * ROWS, :]
        place(out_ref, v, high + low)
    coded = jnp.maximum(acc[4 * ROWS:5 * ROWS, :], 2.0 ** -63)
    power = jnp.floor(jnp.log2(coded) + 63.002)
    fraction = jnp.floor((coded * jnp.exp2(63.0 - power) - 1.0) * 128.0 + 0.5)
    place(out_ref, 2, power * 128.0 + fraction)


def owner_kernel(inbox_ref, pin_hbm, load_hbm, weight_hbm, parent_hbm, delay_ref, reply_ref,
                 upper_s, lower_s, pieces, picks, acc, pin_ref, load_ref, weight_ref, parent_ref, sems):
    copies = copy_all(((pin_hbm, pin_ref), (load_hbm, load_ref), (weight_hbm, weight_ref),
                       (parent_hbm, parent_ref)), sems)
    slot = take(inbox_ref, 2, 6).astype(jnp.int32)
    upper_s[...] = (slot >> 8).astype(F32)
    lower_s[...] = (slot & (HALF - 1)).astype(F32)
    for v in range(2):
        high, low = split(take(inbox_ref, v, 6))
        pieces[2 * v * ROWS:(2 * v + 1) * ROWS, :] = high
        pieces[(2 * v + 1) * ROWS:(2 * v + 2) * ROWS, :] = low
    acc[...] = jnp.zeros_like(acc)
    iota_u = iota_bf(64, CAPS)
    iota_l = iota_bf(HALF, CAPS)
    zero, one = jnp.zeros((), BF), jnp.ones((), BF)
    units = ROWS // 8

    def lower_ones(lower, j):
        return jnp.where(iota_l == spread(lower[j:j + 1, :], HALF), one, zero)

    def collect(u):
        upper, lower = eight(upper_s, u), eight(lower_s, u)
        values = [pieces[pl.ds(pl.multiple_of(p * ROWS + u * 8, 8), 8), :] for p in range(4)]
        for j0 in (0, 4):
            left, right = [], []
            for j in range(j0, j0 + 4):
                hit = iota_u == spread(upper[j:j + 1, :], 64)
                left.append(jnp.concatenate(
                    [jnp.where(hit, spread(v[j:j + 1, :], 64), zero) for v in values], axis=0))
                right.append(lower_ones(lower, j))
            acc[...] += mm(jnp.concatenate(left, axis=1), jnp.concatenate(right, axis=1), NT)

    repeat(units, OWNER_UNITS, collect)
    for copy in copies:
        copy.wait()

    def table(at):
        both = acc[at:at + 64, :] + acc[at + 64:at + 128, :]
        return jnp.concatenate([both[:NODES], both[NODES:]], axis=1)

    cap = load_ref[...] + table(0)
    res = pin_ref[...] + table(128)
    weight = weight_ref[...]
    iota8 = lax.broadcasted_iota(jnp.int32, (8, 2 * HALF), 0)
    tiles = NODES // 8
    cut = lambda a: [a[8 * t:8 * t + 8, :] for t in range(tiles)]
    sub, below, res = cut(cap), cut(weight), cut(res)
    for k in range(NODES - 1, 0, -1):
        t, r = divmod(k, 8)
        parent = jnp.broadcast_to(parent_ref[k:k + 1, :], iota8.shape)
        sub_k = jnp.broadcast_to(sub[t][r:r + 1, :], iota8.shape)
        below_k = jnp.broadcast_to(below[t][r:r + 1, :], iota8.shape)
        for a in range((k - 1) // 8 + 1):
            hit = parent == iota8 + 8 * a
            sub[a] = sub[a] + jnp.where(hit, sub_k, 0.0)
            below[a] = below[a] + jnp.where(hit, below_k, 0.0)
    step_d = [res[t] * sub[t] for t in range(tiles)]
    step_g = [res[t] * below[t] for t in range(tiles)]
    down_d, down_g = list(step_d), list(step_g)
    for k in range(1, NODES):
        t, r = divmod(k, 8)
        parent = jnp.broadcast_to(parent_ref[k:k + 1, :], iota8.shape)
        from_d = from_g = None
        for a in range((k - 1) // 8 + 1):
            hit = parent == iota8 + 8 * a
            d, g = jnp.where(hit, down_d[a], 0.0), jnp.where(hit, down_g[a], 0.0)
            from_d = d if from_d is None else from_d + d
            from_g = g if from_g is None else from_g + g
        here = iota8 == r
        down_d[t] = jnp.where(here, step_d[t] + jnp.sum(from_d, axis=0, keepdims=True), down_d[t])
        down_g[t] = jnp.where(here, step_g[t] + jnp.sum(from_g, axis=0, keepdims=True), down_g[t])
    delay_ref[...] = jnp.concatenate(down_d, axis=0)
    sens = jnp.concatenate(
        [SHEET * (below[t] * sub[t]) + GROUND * down_g[t] for t in range(tiles)], axis=0)
    high, low = split(sens)
    picks[...] = jnp.concatenate(
        [high[:, :HALF], high[:, HALF:], low[:, :HALF], low[:, HALF:]], axis=0).astype(BF)
    iota_uf = lax.broadcasted_iota(jnp.int32, (64, CAPS), 0).astype(F32)

    def answer(u):
        upper, lower = eight(upper_s, u), eight(lower_s, u)
        rows = []
        for j in range(8):
            both = mm(picks[...], lower_ones(lower, j), NN)
            kept = jnp.where(iota_uf == upper[j:j + 1, :], both[:64] + both[64:], 0.0)
            rows.append(jnp.sum(kept, axis=0, keepdims=True))
        reply = jnp.concatenate(rows, axis=0)
        for half in (0, 1):
            reply_ref[pl.ds(u * 16 + half, 8, stride=2), :] = reply[:, half * SEG:(half + 1) * SEG]

    repeat(units, OWNER_UNITS, answer)


def final_kernel(returned_ref, owner_ref, rank_ref, out_ref, picks):
    high, low = split(take(returned_ref, 0, 2))
    picks[...] = jnp.concatenate([high, low], axis=0).astype(BF)
    iota_r = iota_bf(CAPS, 2 * SEG)
    iota_o = lax.broadcasted_iota(jnp.int32, (ROWS, 2 * SEG), 0)
    zero, one = jnp.zeros((), BF), jnp.ones((), BF)

    def pair(rows, j):
        return jnp.concatenate([rows[2 * j:2 * j + 1, :], rows[2 * j + 1:2 * j + 2, :]], axis=1)

    def answer(u):
        rank, owner = eight(rank_ref, u), eight(owner_ref, u)
        rows = []
        for j in range(4):
            ones = jnp.where(iota_r == spread(pair(rank, j), CAPS), one, zero)
            both = mm(picks[...], ones, NN)
            kept = jnp.where(iota_o == pair(owner, j), both[:ROWS] + both[ROWS:], 0.0)
            row = jnp.sum(kept, axis=0, keepdims=True)
            rows += [row[:, :SEG], row[:, SEG:]]
        out_ref[pl.ds(pl.multiple_of(u * 8, 8), 8), :] = jnp.concatenate(rows, axis=0)

    repeat(ROWS // 8, FINAL_UNITS, answer)


def call(kernel, name, outs, in_specs, scratch=(), copies=0, cost=None, limit=VMEM_LIMIT):
    spaces = {"s": pltpu.SMEM, "v": pltpu.VMEM, "h": pltpu.HBM}
    specs = [pl.BlockSpec(memory_space=spaces[letter]) for letter in in_specs]
    scratch_shapes = [pltpu.VMEM(shape, dtype) for shape, dtype in scratch]
    if copies:
        scratch_shapes.append(pltpu.SemaphoreType.DMA((copies,)))
    return pl.pallas_call(
        kernel,
        out_shape=[jax.ShapeDtypeStruct(out, F32) for out in outs],
        in_specs=specs,
        out_specs=[pl.BlockSpec(memory_space=pltpu.VMEM)] * len(outs),
        scratch_shapes=scratch_shapes,
        compiler_params=pltpu.CompilerParams(vmem_limit_bytes=limit),
        cost_estimate=cost and pl.CostEstimate(flops=cost * 10 ** 9, bytes_accessed=0, transcendentals=0),
        name=name,
    )


def exchange(lines_of):
    box = lines_of.reshape(ROWS, 1, -1)
    return lax.all_to_all(box, AXES, split_axis=0, concat_axis=0, tiled=True).reshape(lines_of.shape)


def body(seg_start, seg_len, seg_track, seg_nbr, seg_owner, seg_local, seg_node,
         pin_res, load_cap, crit_weight, net_parent):
    devices = lax.axis_size(AXES)
    in_pair = [(i, i ^ 1) for i in range(devices)]
    between = [(i, i + 1 if i % 2 else i - 1) for i in range(1, devices - 1)]
    I32 = jnp.int32
    owner = seg_owner.reshape(ROWS, SEG)
    square, flat, nets = (ROWS, SEG), (ROWS, CAPS), (NODES, 2 * HALF)
    first = (lax.axis_index(AXES) * ROWS).astype(I32).reshape(1)
    near, far = call(edge_kernel, "edge", [(24, SEG)] * 2, "shhh", copies=6, limit=None)(
        first, seg_start, seg_len, seg_track)
    far = lax.ppermute(far, AXES, between)
    near = lax.ppermute(near, AXES, in_pair)
    rank, = call(rank_kernel, "rank", [square], "v", cost=3)(owner)
    wide = (ROWS + 16, SEG)
    seg_cap, outbox = call(
        couple_kernel, "couple", [square, (6 * ROWS, SEG)], "ssvvvvvvvvv",
        [(wide, F32)] * 4 + [((SEG, 6 * SEG), BF)] + [(square, F32)] * 2 + [((5 * ROWS, CAPS), F32)],
        cost=20,
    )(first, seg_nbr.T, seg_start, seg_len, seg_track, near, far, owner, rank, seg_local, seg_node)
    inbox = exchange(outbox)
    delay, reply = call(
        owner_kernel, "owner", [nets, (2 * ROWS, SEG)], "vhhhh",
        [(flat, F32), (flat, F32), ((4 * ROWS, CAPS), F32), ((ROWS, HALF), BF), ((CAPS, HALF), F32)]
        + [(nets, F32)] * 3 + [(nets, I32)], copies=4, cost=9,
    )(inbox, pin_res, load_cap, crit_weight, net_parent)
    returned = exchange(reply)
    seg_sens, = call(final_kernel, "final", [square], "vvv", [((2 * ROWS, CAPS), BF)], cost=3)(
        returned, owner, rank)
    return seg_cap, delay, seg_sens


def solution(mesh):
    rows, nets = P(AXES, None), P(None, AXES)
    placed = (rows, rows, rows, rows, P(AXES, None, None), rows, rows, nets, nets, nets, nets)
    return jax.shard_map(body, mesh=mesh, in_specs=placed, out_specs=(rows, nets, rows), check_vma=False)
```

```python
import jax
import jax.numpy as jnp
from jax import lax
from jax.experimental import pallas as pl
from jax.experimental.pallas import tpu as pltpu
from jax.sharding import PartitionSpec as P

RIM = 4
GROUND = 0.2
COUPLE = 0.005
SHEET = 0.02
AXES = ("tile", "net")
BF = jnp.bfloat16
F32 = jnp.float32

ROWS = 128
SEG = 128
CAPS = 256
NODES = 32
HALF = 256
VMEM_LIMIT = 24 * 1024 * 1024

RANK_ROWS = 64
COUPLE_STEPS = 4
OWNER_UNITS = 8
FINAL_UNITS = 16

NT = (((1,), (1,)), ((), ()))
NN = (((1,), (0,)), ((), ()))


def mm(left, right, dims):
    return lax.dot_general(left, right, dims, preferred_element_type=F32)


def iota_bf(rows, cols):
    return lax.broadcasted_iota(jnp.int32, (rows, cols), 0).astype(F32).astype(BF)


def spread(row, rows):
    sixteen = jnp.broadcast_to(row, (16, row.shape[1])).astype(BF)
    return jnp.concatenate([sixteen] * (rows // 16), axis=0)


def split(value):
    high = value.astype(BF).astype(F32)
    return high, (value - high).astype(BF).astype(F32)


def repeat(count, together, step):
    def several(h, carry):
        for q in range(together):
            step(h * together + q)
        return carry

    if count == together:
        several(0, 0)
    else:
        lax.fori_loop(0, count // together, several, 0)


def even_device(first_ref):
    return ((first_ref[0] // ROWS) & 1) == 0


def copy_all(pairs, sems):
    copies = [pltpu.make_async_copy(source, target, sems.at[n]) for n, (source, target) in enumerate(pairs)]
    for copy in copies:
        copy.start()
    return copies


def edge_kernel(first_ref, start_hbm, len_hbm, track_hbm, near_ref, far_ref, sems):
    even = even_device(first_ref)
    high = pl.multiple_of(jnp.where(even, ROWS - 8, 0), 8)
    low = pl.multiple_of(jnp.where(even, 0, ROWS - 8), 8)
    pairs = []
    for n, source in enumerate((start_hbm, len_hbm, track_hbm)):
        pairs.append((source.at[pl.ds(low, 8), :], far_ref.at[8 * n:8 * n + 8, :]))
        pairs.append((source.at[pl.ds(high, 8), :], near_ref.at[8 * n:8 * n + 8, :]))
    for copy in copy_all(pairs, sems):
        copy.wait()


def rank_kernel(owner_ref, rank_ref):
    iota = lax.broadcasted_iota(jnp.int32, (ROWS, SEG), 0)
    r0 = lax.broadcasted_iota(jnp.int32, (SEG, 2 * SEG), 0)
    c0 = lax.broadcasted_iota(jnp.int32, (SEG, 2 * SEG), 1)
    upper = jnp.where((r0 <= c0), 1.0, 0.0).astype(BF)

    def step(g, before):
        for j in range(RANK_ROWS):
            b = g * RANK_ROWS + j
            hit = iota == owner_ref[pl.ds(b, 1), :]
            ones = jnp.where(hit, 1.0, 0.0).astype(BF)
            sums = mm(ones, upper, NN)
            placed = jnp.where(hit, sums[:, :SEG] + before, 0.0)
            rank_ref[pl.ds(b, 1), :] = jnp.sum(placed, axis=0, keepdims=True) - 1.0
            before = before + sums[:, SEG:]
        return before

    lax.fori_loop(0, ROWS // RANK_ROWS, step, jnp.zeros((ROWS, SEG), F32))


def split3(value):
    high = value.astype(BF).astype(F32)
    rest = value - high
    middle = rest.astype(BF).astype(F32)
    return [high, middle, rest - middle]


def eight(ref, group):
    return ref[pl.ds(pl.multiple_of(group * 8, 8), 8), :]


def lines(value, half, width):
    return pl.ds(2 * value + half, ROWS, stride=width)


def place(ref, value, array):
    for half in (0, 1):
        ref[lines(value, half, 6), :] = array[:, half * SEG:(half + 1) * SEG]


def take(ref, value, width):
    return jnp.concatenate([ref[lines(value, half, width), :] for half in (0, 1)], axis=1)


def couple_kernel(first_ref, nbr_ref, start_ref, len_ref, track_ref, near_ref, far_ref,
                  owner_ref, rank_ref, local_ref, node_ref, cap_ref, out_ref,
                  s_j, e_j, g_j, f_j, pick, full_a, full_b, acc):
    def fill(at, count, start, length, track):
        s_j[at:at + count, :] = start
        e_j[at:at + count, :] = start + length
        g_j[at:at + count, :] = jnp.exp(2.0 * track)
        f_j[at:at + count, :] = jnp.exp(-track)

    fill(8, ROWS, start_ref[...], len_ref[...], track_ref[...])
    even, near, far = even_device(first_ref), near_ref[...], far_ref[...]
    low, high = jnp.where(even, far, near), jnp.where(even, near, far)
    fill(0, 8, low[0:8, :], low[8:16, :], low[16:24, :])
    fill(8 + ROWS, 8, high[0:8, :], high[8:16, :], high[16:24, :])
    row = lax.broadcasted_iota(jnp.int32, (SEG, 6 * SEG), 0)
    col = lax.broadcasted_iota(jnp.int32, (SEG, 6 * SEG), 1) >> 7
    array = jnp.where(row < 24, 0, jnp.where(row < 48, 1, jnp.where(row < 72, 2, 9)))
    pick[...] = jnp.where((row & 1) * 3 + array == col, 1.0, 0.0).astype(BF)
    pair_of = (lax.broadcasted_iota(jnp.int32, (SEG, SEG), 1) & 7) >> 1
    lane = lax.broadcasted_iota(jnp.int32, (8, SEG), 1)
    iota_o = iota_bf(ROWS, SEG)
    iota_r = iota_bf(CAPS, SEG)
    zero, one = jnp.zeros((), BF), jnp.ones((), BF)
    first = first_ref[0]

    def turn(g, full):
        at = pl.ds(pl.multiple_of(8 + g * 8, 8), 8)
        pieces = split3(s_j[at, :]) + split3(e_j[at, :]) + split3(g_j[at, :])
        turned = jnp.concatenate(pieces + [jnp.zeros((SEG - 72, SEG), F32)], axis=0).T
        full[...] = turned

    def spread_pair(pair, full):
        part = jnp.where(pair_of == pair, full[...], 0.0).astype(BF)
        return mm(part, pick[...], NN)

    def pairs(g, j, full, sums):
        rows = []
        for k in range(4):
            near = jnp.clip(nbr_ref[k, g * 8 + j] - first + 8, 0, ROWS + 15)
            rows.append([
                jnp.broadcast_to(ref[pl.ds(near, 1), :], (8, SEG)) for ref in (s_j, e_j, g_j, f_j)
            ])
        base = (j & 1) * 3 * SEG
        for t in range(SEG // 8):
            part = slice(8 * t, 8 * t + 8)
            si = full[part, base:base + SEG]
            ei = full[part, base + SEG:base + 2 * SEG]
            gi = full[part, base + 2 * SEG:base + 3 * SEG]
            total = None
            for sj, ej, gj, fj in rows:
                common = jnp.maximum(jnp.minimum(ei, ej) - jnp.maximum(si, sj), 0.0)
                term = common * (jnp.minimum(gi, gj) * fj)
                total = term if total is None else total + term
            sums[t] = jnp.where(lane == j, jnp.sum(total, axis=1, keepdims=True), sums[t])

    def values_of(g):
        local, node = eight(local_ref, g), eight(node_ref, g)
        cap_hi, cap_lo = split(eight(cap_ref, g))
        res_hi, res_lo = split(SHEET * eight(len_ref, g))
        slot = ((local >> 8) * NODES + node) * HALF + (local & (HALF - 1))
        power = jnp.exp2(((slot >> 7) - 63).astype(F32))
        return [cap_hi, cap_lo, res_hi, res_lo, power * (1.0 + (slot & 127).astype(F32) * (1.0 / 128))]

    def places(j0, rank):
        return jnp.concatenate(
            [jnp.where(iota_r == spread(rank[j:j + 1, :], CAPS), one, zero) for j in range(j0, j0 + 4)],
            axis=1)

    def send(j0, owner, right, values, low, high):
        left = []
        for j in range(j0, j0 + 4):
            hit = iota_o == spread(owner[j:j + 1, :], ROWS)
            left.append(jnp.concatenate(
                [jnp.where(hit, spread(v[j:j + 1, :], ROWS), zero) for v in values[low:high]], axis=0))
        acc[low * ROWS:high * ROWS, :] += mm(jnp.concatenate(left, axis=1), right, NT)

    def step(g, full, full_next):
        turn(jnp.minimum(g + 1, ROWS // 8 - 1), full_next)
        last = jnp.maximum(g - 1, 0)
        owner = jnp.where(g > 0, eight(owner_ref, last).astype(F32), -1.0)
        rank, values = eight(rank_ref, last), values_of(last)
        sums = [jnp.zeros((8, SEG), F32)] * (SEG // 8)
        for j in range(8):
            if j % 4 == 0:
                right = places(j, rank)
                send(j, owner, right, values, 0, 2)
            if j % 4 == 2:
                send(j - 2, owner, right, values, 2, 5)
            if j % 2 == 0:
                wide = spread_pair(j // 2, full)
            pairs(g, j, wide, sums)
        summed = jnp.concatenate(sums, axis=0).T[:8, :]
        at = pl.ds(pl.multiple_of(g * 8, 8), 8)
        scale = f_j[pl.ds(pl.multiple_of(8 + g * 8, 8), 8), :]
        cap_ref[at, :] = GROUND * len_ref[at, :] + COUPLE * scale * summed

    def several(h, carry):
        for q in range(0, COUPLE_STEPS, 2):
            step(COUPLE_STEPS * h + q, full_a, full_b)
            step(COUPLE_STEPS * h + q + 1, full_b, full_a)
        return carry

    acc[...] = jnp.zeros_like(acc)
    cap_ref[0:8, :] = jnp.zeros((8, SEG), F32)
    turn(0, full_a)
    lax.fori_loop(0, ROWS // 8 // COUPLE_STEPS, several, 0)
    last = ROWS // 8 - 1
    owner, rank, values = eight(owner_ref, last).astype(F32), eight(rank_ref, last), values_of(last)
    for j in range(0, 8, 4):
        send(j, owner, places(j, rank), values, 0, 5)
    for v in range(2):
        high = acc[2 * v * ROWS:(2 * v + 1) * ROWS, :]
        low = acc[(2 * v + 1) * ROWS:(2 * v + 2) * ROWS, :]
        place(out_ref, v, high + low)
    coded = jnp.maximum(acc[4 * ROWS:5 * ROWS, :], 2.0 ** -63)
    power = jnp.floor(jnp.log2(coded) + 63.002)
    fraction = jnp.floor((coded * jnp.exp2(63.0 - power) - 1.0) * 128.0 + 0.5)
    place(out_ref, 2, power * 128.0 + fraction)


def owner_kernel(inbox_ref, pin_hbm, load_hbm, weight_hbm, parent_hbm, delay_ref, reply_ref,
                 upper_s, lower_s, pieces, picks, acc, pin_ref, load_ref, weight_ref, parent_ref, sems):
    copies = copy_all(((pin_hbm, pin_ref), (load_hbm, load_ref), (weight_hbm, weight_ref),
                       (parent_hbm, parent_ref)), sems)
    slot = take(inbox_ref, 2, 6).astype(jnp.int32)
    upper_s[...] = (slot >> 8).astype(F32)
    lower_s[...] = (slot & (HALF - 1)).astype(F32)
    for v in range(2):
        high, low = split(take(inbox_ref, v, 6))
        pieces[2 * v * ROWS:(2 * v + 1) * ROWS, :] = high
        pieces[(2 * v + 1) * ROWS:(2 * v + 2) * ROWS, :] = low
    acc[...] = jnp.zeros_like(acc)
    iota_u = iota_bf(64, CAPS)
    iota_l = iota_bf(HALF, CAPS)
    zero, one = jnp.zeros((), BF), jnp.ones((), BF)
    units = ROWS // 8

    def lower_ones(lower, j):
        return jnp.where(iota_l == spread(lower[j:j + 1, :], HALF), one, zero)

    def collect(u):
        upper, lower = eight(upper_s, u), eight(lower_s, u)
        values = [pieces[pl.ds(pl.multiple_of(p * ROWS + u * 8, 8), 8), :] for p in range(4)]
        for j0 in (0, 4):
            left, right = [], []
            for j in range(j0, j0 + 4):
                hit = iota_u == spread(upper[j:j + 1, :], 64)
                left.append(jnp.concatenate(
                    [jnp.where(hit, spread(v[j:j + 1, :], 64), zero) for v in values], axis=0))
                right.append(lower_ones(lower, j))
            acc[...] += mm(jnp.concatenate(left, axis=1), jnp.concatenate(right, axis=1), NT)

    repeat(units, OWNER_UNITS, collect)
    for copy in copies:
        copy.wait()

    def table(at):
        both = acc[at:at + 64, :] + acc[at + 64:at + 128, :]
        return jnp.concatenate([both[:NODES], both[NODES:]], axis=1)

    cap = load_ref[...] + table(0)
    res = pin_ref[...] + table(128)
    weight = weight_ref[...]
    iota8 = lax.broadcasted_iota(jnp.int32, (8, 2 * HALF), 0)
    tiles = NODES // 8
    cut = lambda a: [a[8 * t:8 * t + 8, :] for t in range(tiles)]
    sub, below, res = cut(cap), cut(weight), cut(res)
    for k in range(NODES - 1, 0, -1):
        t, r = divmod(k, 8)
        parent = jnp.broadcast_to(parent_ref[k:k + 1, :], iota8.shape)
        sub_k = jnp.broadcast_to(sub[t][r:r + 1, :], iota8.shape)
        below_k = jnp.broadcast_to(below[t][r:r + 1, :], iota8.shape)
        for a in range((k - 1) // 8 + 1):
            hit = parent == iota8 + 8 * a
            sub[a] = sub[a] + jnp.where(hit, sub_k, 0.0)
            below[a] = below[a] + jnp.where(hit, below_k, 0.0)
    step_d = [res[t] * sub[t] for t in range(tiles)]
    step_g = [res[t] * below[t] for t in range(tiles)]
    down_d, down_g = list(step_d), list(step_g)
    for k in range(1, NODES):
        t, r = divmod(k, 8)
        parent = jnp.broadcast_to(parent_ref[k:k + 1, :], iota8.shape)
        from_d = from_g = None
        for a in range((k - 1) // 8 + 1):
            hit = parent == iota8 + 8 * a
            d, g = jnp.where(hit, down_d[a], 0.0), jnp.where(hit, down_g[a], 0.0)
            from_d = d if from_d is None else from_d + d
            from_g = g if from_g is None else from_g + g
        here = iota8 == r
        down_d[t] = jnp.where(here, step_d[t] + jnp.sum(from_d, axis=0, keepdims=True), down_d[t])
        down_g[t] = jnp.where(here, step_g[t] + jnp.sum(from_g, axis=0, keepdims=True), down_g[t])
    delay_ref[...] = jnp.concatenate(down_d, axis=0)
    sens = jnp.concatenate(
        [SHEET * (below[t] * sub[t]) + GROUND * down_g[t] for t in range(tiles)], axis=0)
    high, low = split(sens)
    picks[...] = jnp.concatenate(
        [high[:, :HALF], high[:, HALF:], low[:, :HALF], low[:, HALF:]], axis=0).astype(BF)
    iota_uf = lax.broadcasted_iota(jnp.int32, (64, CAPS), 0).astype(F32)

    def answer(u):
        upper, lower = eight(upper_s, u), eight(lower_s, u)
        rows = []
        for j in range(8):
            both = mm(picks[...], lower_ones(lower, j), NN)
            kept = jnp.where(iota_uf == upper[j:j + 1, :], both[:64] + both[64:], 0.0)
            rows.append(jnp.sum(kept, axis=0, keepdims=True))
        reply = jnp.concatenate(rows, axis=0)
        for half in (0, 1):
            reply_ref[pl.ds(u * 16 + half, 8, stride=2), :] = reply[:, half * SEG:(half + 1) * SEG]

    repeat(units, OWNER_UNITS, answer)


def final_kernel(returned_ref, owner_ref, rank_ref, out_ref, picks):
    high, low = split(take(returned_ref, 0, 2))
    picks[...] = jnp.concatenate([high, low], axis=0).astype(BF)
    iota_r = iota_bf(CAPS, 2 * SEG)
    iota_o = lax.broadcasted_iota(jnp.int32, (ROWS, 2 * SEG), 0)
    zero, one = jnp.zeros((), BF), jnp.ones((), BF)

    def pair(rows, j):
        return jnp.concatenate([rows[2 * j:2 * j + 1, :], rows[2 * j + 1:2 * j + 2, :]], axis=1)

    def answer(u):
        rank, owner = eight(rank_ref, u), eight(owner_ref, u)
        rows = []
        for j in range(4):
            ones = jnp.where(iota_r == spread(pair(rank, j), CAPS), one, zero)
            both = mm(picks[...], ones, NN)
            kept = jnp.where(iota_o == pair(owner, j), both[:ROWS] + both[ROWS:], 0.0)
            row = jnp.sum(kept, axis=0, keepdims=True)
            rows += [row[:, :SEG], row[:, SEG:]]
        out_ref[pl.ds(pl.multiple_of(u * 8, 8), 8), :] = jnp.concatenate(rows, axis=0)

    repeat(ROWS // 8, FINAL_UNITS, answer)


def call(kernel, name, outs, in_specs, scratch=(), copies=0, cost=None, limit=VMEM_LIMIT):
    spaces = {"s": pltpu.SMEM, "v": pltpu.VMEM, "h": pltpu.HBM}
    specs = [pl.BlockSpec(memory_space=spaces[letter]) for letter in in_specs]
    scratch_shapes = [pltpu.VMEM(shape, dtype) for shape, dtype in scratch]
    if copies:
        scratch_shapes.append(pltpu.SemaphoreType.DMA((copies,)))
    return pl.pallas_call(
        kernel,
        out_shape=[jax.ShapeDtypeStruct(out, F32) for out in outs],
        in_specs=specs,
        out_specs=[pl.BlockSpec(memory_space=pltpu.VMEM)] * len(outs),
        scratch_shapes=scratch_shapes,
        compiler_params=pltpu.CompilerParams(vmem_limit_bytes=limit),
        cost_estimate=cost and pl.CostEstimate(flops=cost * 10 ** 9, bytes_accessed=0, transcendentals=0),
        name=name,
    )


def exchange(lines_of):
    box = lines_of.reshape(ROWS, 1, -1)
    return lax.all_to_all(box, AXES, split_axis=0, concat_axis=0, tiled=True).reshape(lines_of.shape)


def body(seg_start, seg_len, seg_track, seg_nbr, seg_owner, seg_local, seg_node,
         pin_res, load_cap, crit_weight, net_parent):
    devices = lax.axis_size(AXES)
    in_pair = [(i, i ^ 1) for i in range(devices)]
    between = [(i, i + 1 if i % 2 else i - 1) for i in range(1, devices - 1)]
    I32 = jnp.int32
    owner = seg_owner.reshape(ROWS, SEG)
    square, flat, nets = (ROWS, SEG), (ROWS, CAPS), (NODES, 2 * HALF)
    first = (lax.axis_index(AXES) * ROWS).astype(I32).reshape(1)
    near, far = call(edge_kernel, "edge", [(24, SEG)] * 2, "shhh", copies=6, limit=None)(
        first, seg_start, seg_len, seg_track)
    far = lax.ppermute(far, AXES, between)
    near = lax.ppermute(near, AXES, in_pair)
    rank, = call(rank_kernel, "rank", [square], "v", cost=3)(owner)
    wide = (ROWS + 16, SEG)
    seg_cap, outbox = call(
        couple_kernel, "couple", [square, (6 * ROWS, SEG)], "ssvvvvvvvvv",
        [(wide, F32)] * 4 + [((SEG, 6 * SEG), BF)] + [(square, F32)] * 2 + [((5 * ROWS, CAPS), F32)],
        cost=20,
    )(first, seg_nbr.T, seg_start, seg_len, seg_track, near, far, owner, rank, seg_local, seg_node)
    inbox = exchange(outbox)
    delay, reply = call(
        owner_kernel, "owner", [nets, (2 * ROWS, SEG)], "vhhhh",
        [(flat, F32), (flat, F32), ((4 * ROWS, CAPS), F32), ((ROWS, HALF), BF), ((CAPS, HALF), F32)]
        + [(nets, F32)] * 3 + [(nets, I32)], copies=4, cost=9,
    )(inbox, pin_res, load_cap, crit_weight, net_parent)
    returned = exchange(reply)
    seg_sens, = call(final_kernel, "final", [square], "vvv", [((2 * ROWS, CAPS), BF)], cost=3)(
        returned, owner, rank)
    return seg_cap, delay, seg_sens


def solution(mesh):
    rows, nets = P(AXES, None), P(None, AXES)
    placed = (rows, rows, rows, rows, P(AXES, None, None), rows, rows, nets, nets, nets, nets)
    return jax.shard_map(body, mesh=mesh, in_specs=placed, out_specs=(rows, nets, rows), check_vma=False)
```

```python
import jax
import jax.numpy as jnp
from jax import lax
from jax.experimental import pallas as pl
from jax.experimental.pallas import tpu as pltpu
from jax.sharding import PartitionSpec as P

RIM = 4
GROUND = 0.2
COUPLE = 0.005
SHEET = 0.02
AXES = ("tile", "net")
BF = jnp.bfloat16
F32 = jnp.float32

ROWS = 128
SEG = 128
CAPS = 256
NODES = 32
HALF = 256
VMEM_LIMIT = 24 * 1024 * 1024

RANK_ROWS = 64
COUPLE_STEPS = 4
OWNER_UNITS = 8
FINAL_UNITS = 8

NT = (((1,), (1,)), ((), ()))
NN = (((1,), (0,)), ((), ()))


def mm(left, right, dims):
    return lax.dot_general(left, right, dims, preferred_element_type=F32)


def iota_bf(rows, cols):
    return lax.broadcasted_iota(jnp.int32, (rows, cols), 0).astype(F32).astype(BF)


def spread(row, rows):
    sixteen = jnp.broadcast_to(row, (16, row.shape[1])).astype(BF)
    return jnp.concatenate([sixteen] * (rows // 16), axis=0)


def split(value):
    high = value.astype(BF).astype(F32)
    return high, (value - high).astype(BF).astype(F32)


def repeat(count, together, step):
    def several(h, carry):
        for q in range(together):
            step(h * together + q)
        return carry

    if count == together:
        several(0, 0)
    else:
        lax.fori_loop(0, count // together, several, 0)


def even_device(first_ref):
    return ((first_ref[0] // ROWS) & 1) == 0


def copy_all(pairs, sems):
    copies = [pltpu.make_async_copy(source, target, sems.at[n]) for n, (source, target) in enumerate(pairs)]
    for copy in copies:
        copy.start()
    return copies


def edge_kernel(first_ref, start_hbm, len_hbm, track_hbm, near_ref, far_ref, sems):
    even = even_device(first_ref)
    high = pl.multiple_of(jnp.where(even, ROWS - 8, 0), 8)
    low = pl.multiple_of(jnp.where(even, 0, ROWS - 8), 8)
    pairs = []
    for n, source in enumerate((start_hbm, len_hbm, track_hbm)):
        pairs.append((source.at[pl.ds(low, 8), :], far_ref.at[8 * n:8 * n + 8, :]))
        pairs.append((source.at[pl.ds(high, 8), :], near_ref.at[8 * n:8 * n + 8, :]))
    for copy in copy_all(pairs, sems):
        copy.wait()


def rank_kernel(owner_ref, rank_ref):
    iota = lax.broadcasted_iota(jnp.int32, (ROWS, SEG), 0)
    r0 = lax.broadcasted_iota(jnp.int32, (SEG, 2 * SEG), 0)
    c0 = lax.broadcasted_iota(jnp.int32, (SEG, 2 * SEG), 1)
    upper = jnp.where((r0 <= c0), 1.0, 0.0).astype(BF)

    def step(g, before):
        for j in range(RANK_ROWS):
            b = g * RANK_ROWS + j
            hit = iota == owner_ref[pl.ds(b, 1), :]
            ones = jnp.where(hit, 1.0, 0.0).astype(BF)
            sums = mm(ones, upper, NN)
            placed = jnp.where(hit, sums[:, :SEG] + before, 0.0)
            rank_ref[pl.ds(b, 1), :] = jnp.sum(placed, axis=0, keepdims=True) - 1.0
            before = before + sums[:, SEG:]
        return before

    lax.fori_loop(0, ROWS // RANK_ROWS, step, jnp.zeros((ROWS, SEG), F32))


def split3(value):
    high = value.astype(BF).astype(F32)
    rest = value - high
    middle = rest.astype(BF).astype(F32)
    return [high, middle, rest - middle]


def eight(ref, group):
    return ref[pl.ds(pl.multiple_of(group * 8, 8), 8), :]


def lines(value, half, width):
    return pl.ds(2 * value + half, ROWS, stride=width)


def place(ref, value, array):
    for half in (0, 1):
        ref[lines(value, half, 6), :] = array[:, half * SEG:(half + 1) * SEG]


def take(ref, value, width):
    return jnp.concatenate([ref[lines(value, half, width), :] for half in (0, 1)], axis=1)


def couple_kernel(first_ref, nbr_ref, start_ref, len_ref, track_ref, near_ref, far_ref,
                  owner_ref, rank_ref, local_ref, node_ref, cap_ref, out_ref,
                  s_j, e_j, g_j, f_j, pick, full_a, full_b, acc):
    def fill(at, count, start, length, track):
        s_j[at:at + count, :] = start
        e_j[at:at + count, :] = start + length
        g_j[at:at + count, :] = jnp.exp(2.0 * track)
        f_j[at:at + count, :] = jnp.exp(-track)

    fill(8, ROWS, start_ref[...], len_ref[...], track_ref[...])
    even, near, far = even_device(first_ref), near_ref[...], far_ref[...]
    low, high = jnp.where(even, far, near), jnp.where(even, near, far)
    fill(0, 8, low[0:8, :], low[8:16, :], low[16:24, :])
    fill(8 + ROWS, 8, high[0:8, :], high[8:16, :], high[16:24, :])
    row = lax.broadcasted_iota(jnp.int32, (SEG, 6 * SEG), 0)
    col = lax.broadcasted_iota(jnp.int32, (SEG, 6 * SEG), 1) >> 7
    array = jnp.where(row < 24, 0, jnp.where(row < 48, 1, jnp.where(row < 72, 2, 9)))
    pick[...] = jnp.where((row & 1) * 3 + array == col, 1.0, 0.0).astype(BF)
    pair_of = (lax.broadcasted_iota(jnp.int32, (SEG, SEG), 1) & 7) >> 1
    lane = lax.broadcasted_iota(jnp.int32, (8, SEG), 1)
    iota_o = iota_bf(ROWS, SEG)
    iota_r = iota_bf(CAPS, SEG)
    zero, one = jnp.zeros((), BF), jnp.ones((), BF)
    first = first_ref[0]

    def turn(g, full):
        at = pl.ds(pl.multiple_of(8 + g * 8, 8), 8)
        pieces = split3(s_j[at, :]) + split3(e_j[at, :]) + split3(g_j[at, :])
        turned = jnp.concatenate(pieces + [jnp.zeros((SEG - 72, SEG), F32)], axis=0).T
        full[...] = turned

    def spread_pair(pair, full):
        part = jnp.where(pair_of == pair, full[...], 0.0).astype(BF)
        return mm(part, pick[...], NN)

    def pairs(g, j, full, sums):
        rows = []
        for k in range(4):
            near = jnp.clip(nbr_ref[k, g * 8 + j] - first + 8, 0, ROWS + 15)
            rows.append([
                jnp.broadcast_to(ref[pl.ds(near, 1), :], (8, SEG)) for ref in (s_j, e_j, g_j, f_j)
            ])
        base = (j & 1) * 3 * SEG
        for t in range(SEG // 8):
            part = slice(8 * t, 8 * t + 8)
            si = full[part, base:base + SEG]
            ei = full[part, base + SEG:base + 2 * SEG]
            gi = full[part, base + 2 * SEG:base + 3 * SEG]
            total = None
            for sj, ej, gj, fj in rows:
                common = jnp.maximum(jnp.minimum(ei, ej) - jnp.maximum(si, sj), 0.0)
                term = common * (jnp.minimum(gi, gj) * fj)
                total = term if total is None else total + term
            sums[t] = jnp.where(lane == j, jnp.sum(total, axis=1, keepdims=True), sums[t])

    def values_of(g):
        local, node = eight(local_ref, g), eight(node_ref, g)
        cap_hi, cap_lo = split(eight(cap_ref, g))
        res_hi, res_lo = split(SHEET * eight(len_ref, g))
        slot = ((local >> 8) * NODES + node) * HALF + (local & (HALF - 1))
        power = jnp.exp2(((slot >> 7) - 63).astype(F32))
        return [cap_hi, cap_lo, res_hi, res_lo, power * (1.0 + (slot & 127).astype(F32) * (1.0 / 128))]

    def places(j0, rank):
        return jnp.concatenate(
            [jnp.where(iota_r == spread(rank[j:j + 1, :], CAPS), one, zero) for j in range(j0, j0 + 4)],
            axis=1)

    def send(j0, owner, right, values, low, high):
        left = []
        for j in range(j0, j0 + 4):
            hit = iota_o == spread(owner[j:j + 1, :], ROWS)
            left.append(jnp.concatenate(
                [jnp.where(hit, spread(v[j:j + 1, :], ROWS), zero) for v in values[low:high]], axis=0))
        acc[low * ROWS:high * ROWS, :] += mm(jnp.concatenate(left, axis=1), right, NT)

    def step(g, full, full_next):
        turn(jnp.minimum(g + 1, ROWS // 8 - 1), full_next)
        last = jnp.maximum(g - 1, 0)
        owner = jnp.where(g > 0, eight(owner_ref, last).astype(F32), -1.0)
        rank, values = eight(rank_ref, last), values_of(last)
        sums = [jnp.zeros((8, SEG), F32)] * (SEG // 8)
        for j in range(8):
            if j % 4 == 0:
                right = places(j, rank)
                send(j, owner, right, values, 0, 2)
            if j % 4 == 2:
                send(j - 2, owner, right, values, 2, 5)
            if j % 2 == 0:
                wide = spread_pair(j // 2, full)
            pairs(g, j, wide, sums)
        summed = jnp.concatenate(sums, axis=0).T[:8, :]
        at = pl.ds(pl.multiple_of(g * 8, 8), 8)
        scale = f_j[pl.ds(pl.multiple_of(8 + g * 8, 8), 8), :]
        cap_ref[at, :] = GROUND * len_ref[at, :] + COUPLE * scale * summed

    def several(h, carry):
        for q in range(0, COUPLE_STEPS, 2):
            step(COUPLE_STEPS * h + q, full_a, full_b)
            step(COUPLE_STEPS * h + q + 1, full_b, full_a)
        return carry

    acc[...] = jnp.zeros_like(acc)
    cap_ref[0:8, :] = jnp.zeros((8, SEG), F32)
    turn(0, full_a)
    lax.fori_loop(0, ROWS // 8 // COUPLE_STEPS, several, 0)
    last = ROWS // 8 - 1
    owner, rank, values = eight(owner_ref, last).astype(F32), eight(rank_ref, last), values_of(last)
    for j in range(0, 8, 4):
        send(j, owner, places(j, rank), values, 0, 5)
    for v in range(2):
        high = acc[2 * v * ROWS:(2 * v + 1) * ROWS, :]
        low = acc[(2 * v + 1) * ROWS:(2 * v + 2) * ROWS, :]
        place(out_ref, v, high + low)
    coded = jnp.maximum(acc[4 * ROWS:5 * ROWS, :], 2.0 ** -63)
    power = jnp.floor(jnp.log2(coded) + 63.002)
    fraction = jnp.floor((coded * jnp.exp2(63.0 - power) - 1.0) * 128.0 + 0.5)
    place(out_ref, 2, power * 128.0 + fraction)


def owner_kernel(inbox_ref, pin_hbm, load_hbm, weight_hbm, parent_hbm, delay_ref, reply_ref,
                 upper_s, lower_s, pieces, picks, acc, pin_ref, load_ref, weight_ref, parent_ref, sems):
    copies = copy_all(((pin_hbm, pin_ref), (load_hbm, load_ref), (weight_hbm, weight_ref),
                       (parent_hbm, parent_ref)), sems)
    slot = take(inbox_ref, 2, 6).astype(jnp.int32)
    upper_s[...] = (slot >> 8).astype(F32)
    lower_s[...] = (slot & (HALF - 1)).astype(F32)
    for v in range(2):
        high, low = split(take(inbox_ref, v, 6))
        pieces[2 * v * ROWS:(2 * v + 1) * ROWS, :] = high
        pieces[(2 * v + 1) * ROWS:(2 * v + 2) * ROWS, :] = low
    acc[...] = jnp.zeros_like(acc)
    iota_u = iota_bf(64, CAPS)
    iota_l = iota_bf(HALF, CAPS)
    zero, one = jnp.zeros((), BF), jnp.ones((), BF)
    units = ROWS // 8

    def lower_ones(lower, j):
        return jnp.where(iota_l == spread(lower[j:j + 1, :], HALF), one, zero)

    def collect(u):
        upper, lower = eight(upper_s, u), eight(lower_s, u)
        values = [pieces[pl.ds(pl.multiple_of(p * ROWS + u * 8, 8), 8), :] for p in range(4)]
        for j0 in (0, 4):
            left, right = [], []
            for j in range(j0, j0 + 4):
                hit = iota_u == spread(upper[j:j + 1, :], 64)
                left.append(jnp.concatenate(
                    [jnp.where(hit, spread(v[j:j + 1, :], 64), zero) for v in values], axis=0))
                right.append(lower_ones(lower, j))
            acc[...] += mm(jnp.concatenate(left, axis=1), jnp.concatenate(right, axis=1), NT)

    repeat(units, OWNER_UNITS, collect)
    for copy in copies:
        copy.wait()

    def table(at):
        both = acc[at:at + 64, :] + acc[at + 64:at + 128, :]
        return jnp.concatenate([both[:NODES], both[NODES:]], axis=1)

    cap = load_ref[...] + table(0)
    res = pin_ref[...] + table(128)
    weight = weight_ref[...]
    iota8 = lax.broadcasted_iota(jnp.int32, (8, 2 * HALF), 0)
    tiles = NODES // 8
    cut = lambda a: [a[8 * t:8 * t + 8, :] for t in range(tiles)]
    sub, below, res = cut(cap), cut(weight), cut(res)
    for k in range(NODES - 1, 0, -1):
        t, r = divmod(k, 8)
        parent = jnp.broadcast_to(parent_ref[k:k + 1, :], iota8.shape)
        sub_k = jnp.broadcast_to(sub[t][r:r + 1, :], iota8.shape)
        below_k = jnp.broadcast_to(below[t][r:r + 1, :], iota8.shape)
        for a in range((k - 1) // 8 + 1):
            hit = parent == iota8 + 8 * a
            sub[a] = sub[a] + jnp.where(hit, sub_k, 0.0)
            below[a] = below[a] + jnp.where(hit, below_k, 0.0)
    step_d = [res[t] * sub[t] for t in range(tiles)]
    step_g = [res[t] * below[t] for t in range(tiles)]
    down_d, down_g = list(step_d), list(step_g)
    for k in range(1, NODES):
        t, r = divmod(k, 8)
        parent = jnp.broadcast_to(parent_ref[k:k + 1, :], iota8.shape)
        from_d = from_g = None
        for a in range((k - 1) // 8 + 1):
            hit = parent == iota8 + 8 * a
            d, g = jnp.where(hit, down_d[a], 0.0), jnp.where(hit, down_g[a], 0.0)
            from_d = d if from_d is None else from_d + d
            from_g = g if from_g is None else from_g + g
        here = iota8 == r
        down_d[t] = jnp.where(here, step_d[t] + jnp.sum(from_d, axis=0, keepdims=True), down_d[t])
        down_g[t] = jnp.where(here, step_g[t] + jnp.sum(from_g, axis=0, keepdims=True), down_g[t])
    delay_ref[...] = jnp.concatenate(down_d, axis=0)
    sens = jnp.concatenate(
        [SHEET * (below[t] * sub[t]) + GROUND * down_g[t] for t in range(tiles)], axis=0)
    high, low = split(sens)
    picks[...] = jnp.concatenate(
        [high[:, :HALF], high[:, HALF:], low[:, :HALF], low[:, HALF:]], axis=0).astype(BF)
    iota_uf = lax.broadcasted_iota(jnp.int32, (64, CAPS), 0).astype(F32)

    def answer(u):
        upper, lower = eight(upper_s, u), eight(lower_s, u)
        rows = []
        for j in range(8):
            both = mm(picks[...], lower_ones(lower, j), NN)
            kept = jnp.where(iota_uf == upper[j:j + 1, :], both[:64] + both[64:], 0.0)
            rows.append(jnp.sum(kept, axis=0, keepdims=True))
        reply = jnp.concatenate(rows, axis=0)
        for half in (0, 1):
            reply_ref[pl.ds(u * 16 + half, 8, stride=2), :] = reply[:, half * SEG:(half + 1) * SEG]

    repeat(units, OWNER_UNITS, answer)


def final_kernel(returned_ref, owner_ref, rank_ref, out_ref, picks):
    high, low = split(take(returned_ref, 0, 2))
    picks[...] = jnp.concatenate([high, low], axis=0).astype(BF)
    iota_r = iota_bf(CAPS, 2 * SEG)
    iota_o = lax.broadcasted_iota(jnp.int32, (ROWS, 2 * SEG), 0)
    zero, one = jnp.zeros((), BF), jnp.ones((), BF)

    def pair(rows, j):
        return jnp.concatenate([rows[2 * j:2 * j + 1, :], rows[2 * j + 1:2 * j + 2, :]], axis=1)

    def answer(u):
        rank, owner = eight(rank_ref, u), eight(owner_ref, u)
        rows = []
        for j in range(4):
            ones = jnp.where(iota_r == spread(pair(rank, j), CAPS), one, zero)
            both = mm(picks[...], ones, NN)
            kept = jnp.where(iota_o == pair(owner, j), both[:ROWS] + both[ROWS:], 0.0)
            row = jnp.sum(kept, axis=0, keepdims=True)
            rows += [row[:, :SEG], row[:, SEG:]]
        out_ref[pl.ds(pl.multiple_of(u * 8, 8), 8), :] = jnp.concatenate(rows, axis=0)

    repeat(ROWS // 8, FINAL_UNITS, answer)


def call(kernel, name, outs, in_specs, scratch=(), copies=0, cost=None, limit=VMEM_LIMIT):
    spaces = {"s": pltpu.SMEM, "v": pltpu.VMEM, "h": pltpu.HBM}
    specs = [pl.BlockSpec(memory_space=spaces[letter]) for letter in in_specs]
    scratch_shapes = [pltpu.VMEM(shape, dtype) for shape, dtype in scratch]
    if copies:
        scratch_shapes.append(pltpu.SemaphoreType.DMA((copies,)))
    return pl.pallas_call(
        kernel,
        out_shape=[jax.ShapeDtypeStruct(out, F32) for out in outs],
        in_specs=specs,
        out_specs=[pl.BlockSpec(memory_space=pltpu.VMEM)] * len(outs),
        scratch_shapes=scratch_shapes,
        compiler_params=pltpu.CompilerParams(vmem_limit_bytes=limit),
        cost_estimate=cost and pl.CostEstimate(flops=cost * 10 ** 9, bytes_accessed=0, transcendentals=0),
        name=name,
    )


def exchange(lines_of):
    box = lines_of.reshape(ROWS, 1, -1)
    return lax.all_to_all(box, AXES, split_axis=0, concat_axis=0, tiled=True).reshape(lines_of.shape)


def body(seg_start, seg_len, seg_track, seg_nbr, seg_owner, seg_local, seg_node,
         pin_res, load_cap, crit_weight, net_parent):
    devices = lax.axis_size(AXES)
    in_pair = [(i, i ^ 1) for i in range(devices)]
    between = [(i, i + 1 if i % 2 else i - 1) for i in range(1, devices - 1)]
    I32 = jnp.int32
    owner = seg_owner.reshape(ROWS, SEG)
    square, flat, nets = (ROWS, SEG), (ROWS, CAPS), (NODES, 2 * HALF)
    first = (lax.axis_index(AXES) * ROWS).astype(I32).reshape(1)
    near, far = call(edge_kernel, "edge", [(24, SEG)] * 2, "shhh", copies=6, limit=None)(
        first, seg_start, seg_len, seg_track)
    far = lax.ppermute(far, AXES, between)
    rank, = call(rank_kernel, "rank", [square], "v", cost=3)(owner)
    near, rank = lax.optimization_barrier((near, rank))
    near = lax.ppermute(near, AXES, in_pair)
    wide = (ROWS + 16, SEG)
    seg_cap, outbox = call(
        couple_kernel, "couple", [square, (6 * ROWS, SEG)], "ssvvvvvvvvv",
        [(wide, F32)] * 4 + [((SEG, 6 * SEG), BF)] + [(square, F32)] * 2 + [((5 * ROWS, CAPS), F32)],
        cost=20,
    )(first, seg_nbr.T, seg_start, seg_len, seg_track, near, far, owner, rank, seg_local, seg_node)
    inbox = exchange(outbox)
    delay, reply = call(
        owner_kernel, "owner", [nets, (2 * ROWS, SEG)], "vhhhh",
        [(flat, F32), (flat, F32), ((4 * ROWS, CAPS), F32), ((ROWS, HALF), BF), ((CAPS, HALF), F32)]
        + [(nets, F32)] * 3 + [(nets, I32)], copies=4, cost=9,
    )(inbox, pin_res, load_cap, crit_weight, net_parent)
    returned = exchange(reply)
    seg_sens, = call(final_kernel, "final", [square], "vvv", [((2 * ROWS, CAPS), BF)], cost=3)(
        returned, owner, rank)
    return seg_cap, delay, seg_sens


def solution(mesh):
    rows, nets = P(AXES, None), P(None, AXES)
    placed = (rows, rows, rows, rows, P(AXES, None, None), rows, rows, nets, nets, nets, nets)
    return jax.shard_map(body, mesh=mesh, in_specs=placed, out_specs=(rows, nets, rows), check_vma=False)
```
